32 devices in a mesh: seq: 8 (over z, x), head: 4 (over y, core).
Axes of the slice: x: 2, y: 2, z: 4, core: 2. Of those that a mesh axis runs over, the one named last changes fastest.
Arguments:
- patch_tokens: bfloat16 [32, 256, 3072], P('seq'), may hold values from -26 to 26
- projection: bfloat16 [3072, 2, 3, 1536], P(None, None, None, 'head'), may hold values from -0.14433757 to 0.14433757
Outputs:
- space_out: bfloat16 [32, 256, 1536], P('seq', None, 'head')
- time_out: bfloat16 [32, 256, 1536], P('seq', None, 'head')
- clip_factor: float32 [2, 12], P(None, 'head')
The draws below stay inside these ranges and needn't reach their ends.
All inputs are finite; a program needn't handle non-finite values.
Results may differ from the reference program's by a relative error of at most 0.0085.
The reference program's roundings to bfloat16 on the way count: a program that leaves them out, or rounds other values in their place, can miss the bound.
Values may be sent and summed in bfloat16 or wider, within the bound.
No kernel may reach another device: no remote copies, remote signals or barrier semaphores. Data moves between devices by JAX's collectives and lax.ppermute only.
A program may use at most 192 MiB of HBM per device.

```python
import math
import jax
import jax.numpy as jnp
from jax import lax

D = 3072
HL = 12
HD = 128
P_SIZE = 256
FRAMES = 32


def draw_patch_tokens(key, part):
    frame_place = jnp.arange(FRAMES, dtype=jnp.float32) / (FRAMES - 1)
    patch_place = jnp.arange(P_SIZE, dtype=jnp.float32) / (P_SIZE - 1)
    rising = 0.75
    base = jax.random.truncated_normal(key, -5.0, 5.0, (FRAMES, P_SIZE, D), jnp.float32)
    factor = (1.0 + rising * frame_place)[:, None, None] * (1.0 + rising * patch_place)[None, :, None]
    return (base * factor).astype(jnp.bfloat16)


def draw_projection(key, part):
    base = jax.random.truncated_normal(key, -5.0, 5.0, (D, 2, 3, HL, HD), jnp.float32) / math.sqrt(D)
    gains = jnp.exp(jax.random.uniform(jax.random.fold_in(key, 11), (1, 2, 1, HL, 1), jnp.float32, math.log(0.3), math.log(1.5)))
    query_role = (jnp.arange(3) == 0)[None, None, :, None, None]
    factor = jnp.where(query_role, gains, 1.0)
    return (base * factor).reshape(D, 2, 3, HL * HD).astype(jnp.bfloat16)


def setup_inputs(seed: int = 0) -> dict:
    streams_of = jax.random.split(jax.random.key(seed), 3)
    return {
        "patch_tokens": draw_patch_tokens(jax.random.fold_in(streams_of[2], 71), 0),
        "projection": draw_projection(jax.random.fold_in(streams_of[2], 71), 0),
    }


clip_limit = 30.0

def mixing(scores):
    highest = lax.optimization_barrier(jnp.max(scores, axis=-1, keepdims=True))
    expon = jnp.exp(scores - highest)
    return (expon / lax.optimization_barrier(jnp.sum(expon, axis=-1, keepdims=True))).astype(jnp.bfloat16)

def attend_block(block):
    score_scale = 1.0 / math.sqrt(HD)
    query_part = block[:, 0].astype(jnp.float32)
    key_part = block[:, 1].astype(jnp.float32)
    value_part = block[:, 2].astype(jnp.float32)
    scores = jnp.einsum('ihd,jhd->hij', query_part, key_part) * score_scale
    highest = lax.optimization_barrier(jnp.max(scores, axis=(1, 2)))
    weights = mixing(scores).astype(jnp.float32)
    result = jnp.einsum('hij,jhd->ihd', weights, value_part).astype(jnp.bfloat16)
    return (result.reshape(block.shape[0], HL * HD), highest)

def reference(patch_tokens, projection):
    parts = jnp.dot(patch_tokens.reshape(FRAMES * P_SIZE, D), projection.reshape(D, 6 * HL * HD), preferred_element_type=jnp.float32)
    parts = parts.astype(jnp.bfloat16).reshape(FRAMES, P_SIZE, 2, 3, HL, HD)
    space_out, space_high = lax.map(attend_block, parts[:, :, 0])
    time_parts = jnp.swapaxes(parts[:, :, 1], 0, 1)
    time_swapped, time_high = lax.map(attend_block, time_parts)
    time_out = jnp.swapaxes(time_swapped, 0, 1)
    peak = jnp.stack([lax.optimization_barrier(jnp.max(space_high, axis=0)), lax.optimization_barrier(jnp.max(time_high, axis=0))])
    clip_factor = jnp.sqrt(clip_limit / jnp.maximum(peak, clip_limit))
    return (space_out, time_out, clip_factor)
```

```python
import math

import jax
import jax.numpy as jnp
from jax import lax
from jax.experimental import pallas as pl
from jax.experimental.pallas import tpu as pltpu
from jax.sharding import PartitionSpec as P

HD = 128
ROLES = 3
clip_limit = 30.0
score_scale = 1.0 / math.sqrt(HD)
exp_scale = score_scale * math.log2(math.e)
VMEM = pl.BlockSpec(memory_space=pltpu.VMEM)
PARAMS = pltpu.CompilerParams(vmem_limit_bytes=48 * 1024 * 1024)


def dot_nt(a, b):
    return lax.dot_general(a, b, (((1,), (1,)), ((), ())), preferred_element_type=jnp.float32)


def attend(query_part, key_part, value_part, mask=None):
    raw = dot_nt(query_part, key_part)
    if mask is not None:
        raw = jnp.where(mask, raw, -jnp.inf)
    highest = jnp.max(raw, axis=-1, keepdims=True)
    expon = jnp.exp2((raw - highest) * exp_scale)
    weights = (expon * (1.0 / jnp.sum(expon, axis=-1, keepdims=True))).astype(jnp.bfloat16)
    result = jnp.dot(weights, value_part, preferred_element_type=jnp.float32)
    return result, jnp.max(highest, axis=0, keepdims=True)


def space_kernel(heads, x_ref, w_ref, out_ref, peak_ref):
    frame = pl.program_id(0)
    parts = jnp.dot(x_ref[0], w_ref[...], preferred_element_type=jnp.float32).astype(jnp.bfloat16)
    width = heads * HD

    @pl.when(frame == 0)
    def _():
        peak_ref[...] = jnp.full(peak_ref.shape, -jnp.inf, jnp.float32)

    for h in range(heads):
        cols = [parts[:, r * width + h * HD : r * width + (h + 1) * HD] for r in range(ROLES)]
        result, highest = attend(*cols)
        out_ref[0, :, h * HD : (h + 1) * HD] = result.astype(jnp.bfloat16)
        cell = peak_ref.at[:, h * HD : (h + 1) * HD]
        cell[...] = jnp.maximum(cell[...], highest * score_scale)


def space_attention(tokens, weights, heads):
    frames, positions, depth = tokens.shape
    cols = weights.shape[1]
    width = heads * HD
    return pl.pallas_call(
        lambda *refs: space_kernel(heads, *refs),
        grid=(frames,),
        in_specs=[
            pl.BlockSpec((1, positions, depth), lambda f: (f, 0, 0)),
            pl.BlockSpec((depth, cols), lambda f: (0, 0)),
        ],
        out_specs=(
            pl.BlockSpec((1, positions, width), lambda f: (f, 0, 0)),
            pl.BlockSpec((8, width), lambda f: (0, 0)),
        ),
        out_shape=(
            jax.ShapeDtypeStruct((frames, positions, width), jnp.bfloat16),
            jax.ShapeDtypeStruct((8, width), jnp.float32),
        ),
        compiler_params=PARAMS,
        cost_estimate=pl.CostEstimate(
            flops=2 * frames * positions * depth * cols,
            bytes_accessed=2 * (frames * positions * depth + depth * cols),
            transcendentals=frames * heads * positions * positions,
        ),
        name="space_attention",
    )(tokens, weights)


def project_kernel(blocks, rows, x0, x1, x2, x3, w_ref, out_ref):
    groups = rows // 8
    for pair, (one, two) in enumerate(((x0, x1), (x2, x3))):
        both = [
            jnp.dot(x[...].reshape(blocks * rows, x.shape[-1]), w_ref[...], preferred_element_type=jnp.float32)
            for x in (one, two)
        ]
        for b in range(blocks):
            for g in range(groups):
                at = b * rows + g * 8
                tile = jnp.concatenate([y[at : at + 8] for y in both], axis=0)
                start = (pair * blocks + b) * 16
                out_ref[g, start : start + 16, :] = tile.astype(jnp.bfloat16)


def project(sources, weights):
    blocks, rows, depth = sources[0].shape
    cols = weights.shape[1]
    step = cols // ROLES
    whole = pl.BlockSpec((blocks, rows, depth), lambda c: (0, 0, 0))
    groups = rows // 8
    return pl.pallas_call(
        lambda *refs: project_kernel(blocks, rows, *refs),
        grid=(ROLES,),
        in_specs=[whole] * 4 + [pl.BlockSpec((depth, step), lambda c: (1, c))],
        out_specs=pl.BlockSpec((groups, blocks * 32, step), lambda c: (0, 0, c)),
        out_shape=jax.ShapeDtypeStruct((groups, blocks * 32, cols), jnp.bfloat16),
        compiler_params=PARAMS,
        cost_estimate=pl.CostEstimate(
            flops=8 * blocks * rows * depth * cols,
            bytes_accessed=2 * (4 * blocks * rows * depth + depth * cols),
            transcendentals=0,
        ),
        name="project",
    )(*sources, weights)


def pieces(value):
    high = value.astype(jnp.bfloat16).astype(jnp.float32)
    mid = (value - high).astype(jnp.bfloat16).astype(jnp.float32)
    return high, mid, value - high - mid


def time_kernel(heads, sizes, *refs):
    ins, space_peak, outs = refs[: len(sizes)], refs[len(sizes)], refs[len(sizes) + 1 :]
    groups = ins[0].shape[0]
    width = heads * HD
    total = sum(sizes) * 32
    row = lax.broadcasted_iota(jnp.int32, (total, total), 0)
    col = lax.broadcasted_iota(jnp.int32, (total, total), 1)
    mask = ((row ^ col) & 7) == 0
    line = lax.broadcasted_iota(jnp.int32, (16, HD), 0)
    for h in range(heads):
        peak = jnp.full((1, 1), -jnp.inf, jnp.float32)
        for g in range(groups):
            cols = []
            for r in range(ROLES):
                at = r * width + h * HD
                cols.append(jnp.concatenate([x[g, :, at : at + HD] for x in ins], axis=0))
            result, highest = attend(*cols, mask)
            peak = jnp.maximum(peak, highest * score_scale)
            result = result.astype(jnp.bfloat16)
            base, which = 0, 0
            for size in sizes:
                for b in range(size):
                    for pair in range(2):
                        at = base + (pair * size + b) * 16
                        spot = g * 32 + pair * 16
                        outs[which + b][spot : spot + 16, h * HD : (h + 1) * HD] = result[at : at + 16]
                base += size * 32
                which += size
        tail = jnp.zeros((16, HD), jnp.float32)
        mine = space_peak[0:1, h * HD : (h + 1) * HD]
        for i, value in enumerate(pieces(mine) + pieces(jnp.broadcast_to(peak, (1, HD)))):
            tail = jnp.where(line == i, value, tail)
        for out in outs:
            out[groups * 32 : groups * 32 + 16, h * HD : (h + 1) * HD] = tail.astype(jnp.bfloat16)


def time_attention(parts, space_peak, heads):
    sizes = [p.shape[1] // 32 for p in parts]
    groups = parts[0].shape[0]
    width = heads * HD
    total = sum(sizes) * 32
    shape = jax.ShapeDtypeStruct((groups * 32 + 16, width), jnp.bfloat16)
    return pl.pallas_call(
        lambda *refs: time_kernel(heads, sizes, *refs),
        in_specs=[VMEM] * (len(parts) + 1),
        out_specs=[VMEM] * sum(sizes),
        out_shape=[shape] * sum(sizes),
        compiler_params=PARAMS,
        cost_estimate=pl.CostEstimate(
            flops=4 * groups * heads * total * total * HD,
            bytes_accessed=8 * groups * total * width,
            transcendentals=groups * heads * total * total,
        ),
        name="time_attention",
    )(*parts, space_peak)


def finish_kernel(frames_of, heads, index_ref, *refs):
    ins, out_ref, clip_ref = refs[:-2], refs[-2], refs[-1]
    groups = (ins[0].shape[0] - 16) // 32
    me, mine = index_ref[0], index_ref[1]
    peak = None
    for d, source in enumerate(ins):
        for two in range(groups // 2):
            for pair in range(2):
                a, b = (
                    source[(2 * two + k) * 32 + pair * 16 : (2 * two + k) * 32 + pair * 16 + 16, :].astype(jnp.float32)
                    for k in range(2)
                )
                for k in range(2):
                    tile = jnp.concatenate([a[8 * k : 8 * k + 8], b[8 * k : 8 * k + 8]], axis=0)
                    frame = mine ^ frames_of[2 * pair + k]
                    start = pl.multiple_of((me ^ d) * (groups * 8) + two * 16, 16)
                    out_ref[frame, pl.ds(start, 16), :] = tile.astype(jnp.bfloat16)
        tail = source[groups * 32 : groups * 32 + 16, :].astype(jnp.float32)
        values = [tail[3 * a : 3 * a + 1] + tail[3 * a + 1 : 3 * a + 2] + tail[3 * a + 2 : 3 * a + 3] for a in range(2)]
        peak = values if peak is None else [jnp.maximum(p, v) for p, v in zip(peak, values)]
    for a in range(2):
        clip_ref[a : a + 1, :] = jnp.sqrt(clip_limit / jnp.maximum(peak[a], clip_limit))


def finish(index, received, frames, positions, width, frames_of, heads):
    return pl.pallas_call(
        lambda *refs: finish_kernel(frames_of, heads, *refs),
        in_specs=[pl.BlockSpec(memory_space=pltpu.SMEM)] + [VMEM] * len(received),
        out_specs=[VMEM, VMEM],
        out_shape=[
            jax.ShapeDtypeStruct((frames, positions, width), jnp.bfloat16),
            jax.ShapeDtypeStruct((2, width), jnp.float32),
        ],
        compiler_params=PARAMS,
        name="finish",
    )(index, *received)


def swap(value, axis, size, distance):
    return lax.ppermute(value, axis, [(i, i ^ distance) for i in range(size)])


def fast_body(seq, head, patch_tokens, projection):
    frames, positions, depth = patch_tokens.shape
    heads = projection.shape[-1] // HD
    width = heads * HD
    rows = positions // seq
    me, mine = lax.axis_index("seq"), lax.axis_index("head")
    frames_of = (0, 2, 1, 3)

    def piece(frame, owner):
        return lax.dynamic_slice(patch_tokens, (frame, owner * rows, 0), (1, rows, depth))

    got = {d: swap(piece(mine, me ^ d), "seq", seq, d) for d in (4, 5, 6, 7, 2, 3, 1)}
    weights = jnp.transpose(projection, (1, 0, 2, 3)).reshape(2 * depth, ROLES * width)

    own = [piece(mine ^ f, me) for f in frames_of]
    space_out, space_peak = space_attention(patch_tokens, weights, heads)
    parts = [project(own, weights)]
    order = [0]
    for group in ((1, 2, 3), (4, 5, 6, 7)):
        here = jnp.concatenate([got[d] for d in group], axis=0)
        there = swap(here, "head", head, 2)
        sources = (here, there, swap(here, "head", head, 1), swap(there, "head", head, 1))
        parts.append(project(sources, weights))
        order += list(group)
    outs = time_attention(parts, space_peak, heads)
    received = [out if d == 0 else swap(out, "seq", seq, d) for d, out in zip(order, outs)]
    index = jnp.stack([me, mine]).astype(jnp.int32)
    time_out, clip = finish(index, received, frames, positions, width, frames_of, heads)
    return space_out, time_out, clip[:, ::HD]


def mixing(scores):
    highest = jnp.max(scores, axis=-1, keepdims=True)
    expon = jnp.exp(scores - highest)
    return (expon / jnp.sum(expon, axis=-1, keepdims=True)).astype(jnp.bfloat16)


def plain_attention(form, query_part, key_part, value_part):
    scores = jnp.einsum(form[0], query_part, key_part, preferred_element_type=jnp.float32) * score_scale
    result = jnp.einsum(form[1], mixing(scores), value_part, preferred_element_type=jnp.float32)
    return result.astype(jnp.bfloat16), jnp.max(scores, axis=(0, 2, 3))


def plain_body(patch_tokens, projection):
    frames, positions, depth = patch_tokens.shape
    heads = projection.shape[-1] // HD
    parts = jnp.dot(
        patch_tokens.reshape(-1, depth), projection.reshape(depth, -1), preferred_element_type=jnp.float32
    )
    parts = parts.astype(jnp.bfloat16).reshape(frames, positions, 2, ROLES, heads, HD)
    space_out, space_high = plain_attention(
        ("fihd,fjhd->fhij", "fhij,fjhd->fihd"), *(parts[:, :, 0, r] for r in range(ROLES))
    )
    moved = [lax.all_to_all(parts[:, :, 1, r], "seq", split_axis=1, concat_axis=0, tiled=True) for r in range(ROLES)]
    time_out, time_high = plain_attention(("fphd,gphd->phfg", "phfg,gphd->fphd"), *moved)
    time_out = lax.all_to_all(time_out, "seq", split_axis=0, concat_axis=1, tiled=True)
    peak = lax.pmax(jnp.stack([space_high, time_high]), "seq")
    clip_factor = jnp.sqrt(clip_limit / jnp.maximum(peak, clip_limit))
    flat = (frames, positions, heads * HD)
    return space_out.reshape(flat), time_out.reshape(flat), clip_factor


def solution(mesh):
    seq, head = mesh.shape["seq"], mesh.shape["head"]

    def body(patch_tokens, projection):
        frames, positions, _ = patch_tokens.shape
        if seq == 8 and head == 4 and frames == 4 and positions % (16 * seq) == 0:
            return fast_body(seq, head, patch_tokens, projection)
        return plain_body(patch_tokens, projection)

    return jax.shard_map(
        body,
        mesh=mesh,
        in_specs=(P("seq", None, None), P(None, None, None, "head")),
        out_specs=(P("seq", None, "head"), P("seq", None, "head"), P(None, "head")),
        check_vma=False,
    )
```

```python
import math

import jax
import jax.numpy as jnp
from jax import lax
from jax.experimental import pallas as pl
from jax.experimental.pallas import tpu as pltpu
from jax.sharding import PartitionSpec as P

HD = 128
ROLES = 3
clip_limit = 30.0
score_scale = 1.0 / math.sqrt(HD)
exp_scale = score_scale * math.log2(math.e)
VMEM = pl.BlockSpec(memory_space=pltpu.VMEM)
PARAMS = pltpu.CompilerParams(vmem_limit_bytes=48 * 1024 * 1024)


def dot_nt(a, b):
    return lax.dot_general(a, b, (((1,), (1,)), ((), ())), preferred_element_type=jnp.float32)


def attend(query_part, key_part, value_part, mask=None):
    raw = dot_nt(query_part, key_part)
    if mask is not None:
        raw = jnp.where(mask, raw, -jnp.inf)
    highest = jnp.max(raw, axis=-1, keepdims=True)
    expon = jnp.exp2((raw - highest) * exp_scale)
    weights = (expon * (1.0 / jnp.sum(expon, axis=-1, keepdims=True))).astype(jnp.bfloat16)
    result = jnp.dot(weights, value_part, preferred_element_type=jnp.float32)
    return result, jnp.max(highest, axis=0, keepdims=True)


def pick_matrix(which, chunk):
    rows = lax.broadcasted_iota(jnp.int32, (ROLES * chunk, ROLES * 2 * chunk), 0)
    cols = lax.broadcasted_iota(jnp.int32, (ROLES * chunk, ROLES * 2 * chunk), 1)
    source = ((rows % chunk) * ROLES + rows // chunk) * 2 + which
    return jnp.where(cols == source, 1.0, 0.0).astype(jnp.bfloat16)


def pick(pick_ref, w_ref, out_ref):
    depth, _, _, width = w_ref.shape
    chunk = pick_ref.shape[0] // ROLES
    span = 2 * ROLES * chunk
    flat = w_ref.reshape(depth * ROLES * 2, width)
    for i in range(depth // chunk):
        found = jnp.dot(pick_ref[...], flat[i * span : (i + 1) * span, :], preferred_element_type=jnp.float32)
        found = found.astype(jnp.bfloat16)
        for r in range(ROLES):
            out_ref[i * chunk : (i + 1) * chunk, r * width : (r + 1) * width] = found[r * chunk : (r + 1) * chunk]


def pair_rows(one, two, blocks, rows, store):
    for b in range(blocks):
        for g in range(rows // 8):
            at = b * rows + g * 8
            tile = jnp.concatenate([one[at : at + 8], two[at : at + 8]], axis=0)
            store(b, g, tile.astype(jnp.bfloat16))


def early_kernel(count, index_ref, *refs):
    xs, w_ref, weights_ref = refs[:count], refs[count], refs[count + 1]
    outs, (pick_ref, total) = refs[count + 2 : -2], refs[-2:]
    step = pl.program_id(0)

    @pl.when(step == 0)
    def _():
        pick_ref[...] = pick_matrix(1, CHUNK)
        total[...] = jnp.zeros_like(total)

    pick(pick_ref, w_ref, weights_ref)
    frames, rows, block = xs[0].shape
    tokens = jnp.concatenate([x[...].reshape(frames * rows, block) for x in xs], axis=0)
    total[...] += jnp.dot(tokens, weights_ref[...], preferred_element_type=jnp.float32)

    @pl.when(step == pl.num_programs(0) - 1)
    def _():
        for i, out in enumerate(outs):
            for pair in range(frames // 2):
                at = (i * frames + 2 * pair) * rows

                def store(b, g, tile):
                    out[g, pair * 16 : pair * 16 + 16, :] = tile

                pair_rows(total[at : at + rows], total[at + rows : at + 2 * rows], 1, rows, store)


CHUNK = 64


def early(index, tokens, paired, rows, count):
    frames, _, depth = tokens.shape
    width = paired.shape[-1]
    cols = ROLES * width
    block = 512
    out = jax.ShapeDtypeStruct((rows // 8, frames * 8, cols), jnp.bfloat16)
    return pl.pallas_call(
        lambda *refs: early_kernel(count, *refs),
        grid_spec=pltpu.PrefetchScalarGridSpec(
            num_scalar_prefetch=1,
            grid=(depth // block,),
            in_specs=[
                pl.BlockSpec((frames, rows, block), lambda k, index, i=i: (0, index[i], k)) for i in range(count)
            ]
            + [pl.BlockSpec((block, ROLES, 2, width), lambda k, index: (k, 0, 0, 0))],
            out_specs=[pl.BlockSpec((block, cols), lambda k, index: (k, 0))]
            + [pl.BlockSpec(out.shape, lambda k, index: (0, 0, 0))] * count,
            scratch_shapes=[
                pltpu.VMEM((ROLES * CHUNK, 2 * ROLES * CHUNK), jnp.bfloat16),
                pltpu.VMEM((count * frames * rows, cols), jnp.float32),
            ],
        ),
        out_shape=[jax.ShapeDtypeStruct((depth, cols), jnp.bfloat16)] + [out] * count,
        compiler_params=PARAMS,
        cost_estimate=pl.CostEstimate(
            flops=2 * count * frames * rows * depth * cols + 12 * CHUNK * depth * cols,
            bytes_accessed=6 * depth * cols,
            transcendentals=0,
        ),
        name="early",
    )(index, *[tokens] * count, paired)


def space_peak_kernel(heads, x_ref, w_ref, parts_ref, last_ref, peak_ref, pick_ref, weights_ref, total):
    step = pl.program_id(0)
    frames, positions, block = x_ref.shape
    width = heads * HD

    @pl.when(step == 0)
    def _():
        pick_ref[...] = pick_matrix(0, CHUNK)
        total[...] = jnp.zeros_like(total)

    pick(pick_ref, w_ref, weights_ref)
    last_ref[...] = weights_ref[:, 2 * width :]
    tokens = x_ref[...].reshape(frames * positions, block)
    total[...] += jnp.dot(tokens, weights_ref[:, : 2 * width], preferred_element_type=jnp.float32)

    @pl.when(step == pl.num_programs(0) - 1)
    def _():
        parts_ref[...] = total[...].astype(jnp.bfloat16)
        for h in range(heads):
            peak = jnp.full((1, 1), -jnp.inf, jnp.float32)
            for f in range(frames):
                query_part, key_part = (
                    parts_ref[f * positions : (f + 1) * positions, r * width + h * HD : r * width + (h + 1) * HD]
                    for r in range(2)
                )
                peak = jnp.maximum(peak, jnp.max(dot_nt(query_part, key_part), keepdims=True))
            peak_ref[:, h * HD : (h + 1) * HD] = jnp.broadcast_to(peak * score_scale, (8, HD))


def space_peak(tokens, paired, heads):
    frames, positions, depth = tokens.shape
    width = heads * HD
    block = 512
    rows = frames * positions
    return pl.pallas_call(
        lambda *refs: space_peak_kernel(heads, *refs),
        grid=(depth // block,),
        in_specs=[
            pl.BlockSpec((frames, positions, block), lambda k: (0, 0, k)),
            pl.BlockSpec((block, ROLES, 2, width), lambda k: (k, 0, 0, 0)),
        ],
        out_specs=[
            pl.BlockSpec((rows, 2 * width), lambda k: (0, 0)),
            pl.BlockSpec((block, width), lambda k: (k, 0)),
            pl.BlockSpec((8, width), lambda k: (0, 0)),
        ],
        out_shape=[
            jax.ShapeDtypeStruct((rows, 2 * width), jnp.bfloat16),
            jax.ShapeDtypeStruct((depth, width), jnp.bfloat16),
            jax.ShapeDtypeStruct((8, width), jnp.float32),
        ],
        scratch_shapes=[
            pltpu.VMEM((ROLES * CHUNK, 2 * ROLES * CHUNK), jnp.bfloat16),
            pltpu.VMEM((block, ROLES * width), jnp.bfloat16),
            pltpu.VMEM((rows, 2 * width), jnp.float32),
        ],
        compiler_params=PARAMS,
        cost_estimate=pl.CostEstimate(
            flops=4 * rows * depth * width + 12 * CHUNK * depth * ROLES * width,
            bytes_accessed=2 * rows * depth + 14 * depth * width,
            transcendentals=0,
        ),
        name="space_peak",
    )(tokens, paired)


def space_kernel(heads, x_ref, w_ref, parts_ref, out_ref):
    frames, positions, depth = x_ref.shape
    width = heads * HD
    tokens = x_ref[...].reshape(frames * positions, depth)
    values = jnp.dot(tokens, w_ref[...], preferred_element_type=jnp.float32).astype(jnp.bfloat16)
    for f in range(frames):
        rows = slice(f * positions, (f + 1) * positions)
        for h in range(heads):
            cols = [parts_ref[rows, r * width + h * HD : r * width + (h + 1) * HD] for r in range(2)]
            result, _ = attend(*cols, values[rows, h * HD : (h + 1) * HD])
            out_ref[f, :, h * HD : (h + 1) * HD] = result.astype(jnp.bfloat16)


def space_attention(tokens, weights, parts, heads):
    frames, positions, depth = tokens.shape
    width = heads * HD
    block = 2
    return pl.pallas_call(
        lambda *refs: space_kernel(heads, *refs),
        grid=(frames // block,),
        in_specs=[
            pl.BlockSpec((block, positions, depth), lambda f: (f, 0, 0)),
            pl.BlockSpec((depth, width), lambda f: (0, 0)),
            pl.BlockSpec((block * positions, 2 * width), lambda f: (f, 0)),
        ],
        out_specs=pl.BlockSpec((block, positions, width), lambda f: (f, 0, 0)),
        out_shape=jax.ShapeDtypeStruct((frames, positions, width), jnp.bfloat16),
        compiler_params=PARAMS,
        cost_estimate=pl.CostEstimate(
            flops=2 * frames * positions * depth * width,
            bytes_accessed=2 * (frames * positions * depth + depth * width),
            transcendentals=frames * heads * positions * positions,
        ),
        name="space_attention",
    )(tokens, weights, parts)


def project_kernel(blocks, rows, one_ref, two_ref, w_ref, out_ref, held, sems):
    here = blocks * rows

    @pl.when(pl.program_id(0) == 0)
    def _():
        copies = [
            pltpu.make_async_copy(source, held.at[pl.ds(i * here, here)], sems.at[i])
            for i, source in enumerate((one_ref, two_ref))
        ]
        for copy in copies:
            copy.start()
        for copy in copies:
            copy.wait()

    result = jnp.dot(held[...], w_ref[...], preferred_element_type=jnp.float32)

    def store(b, g, tile):
        out_ref[g, b * 16 : b * 16 + 16, :] = tile

    pair_rows(result[:here], result[here:], blocks, rows, store)


def project(one, two, weights):
    blocks, rows, depth = one.shape
    cols = weights.shape[1]
    step = cols // ROLES
    groups = rows // 8
    return pl.pallas_call(
        lambda *refs: project_kernel(blocks, rows, *refs),
        grid=(ROLES,),
        in_specs=[pl.BlockSpec(memory_space=pl.ANY)] * 2 + [pl.BlockSpec((depth, step), lambda r: (0, r))],
        out_specs=pl.BlockSpec((groups, blocks * 16, step), lambda r: (0, 0, r)),
        out_shape=jax.ShapeDtypeStruct((groups, blocks * 16, cols), jnp.bfloat16),
        scratch_shapes=[pltpu.VMEM((2 * blocks * rows, depth), jnp.bfloat16), pltpu.SemaphoreType.DMA((2,))],
        compiler_params=PARAMS,
        cost_estimate=pl.CostEstimate(
            flops=4 * blocks * rows * depth * cols,
            bytes_accessed=2 * (2 * blocks * rows * depth + depth * cols),
            transcendentals=0,
        ),
        name="project",
    )(*[source.reshape(blocks * rows, depth) for source in (one, two)], weights)


def pieces(value):
    high = value.astype(jnp.bfloat16).astype(jnp.float32)
    mid = (value - high).astype(jnp.bfloat16).astype(jnp.float32)
    return high, mid, value - high - mid


def time_kernel(heads, spots, *refs):
    ins, peak_ref, outs = refs[: len(spots)], refs[len(spots)], refs[len(spots) + 1 :]
    groups = ins[0].shape[0]
    width = heads * HD
    total = sum(16 * len(spot) for spot in spots)
    row = lax.broadcasted_iota(jnp.int32, (total, total), 0)
    col = lax.broadcasted_iota(jnp.int32, (total, total), 1)
    mask = ((row ^ col) & 7) == 0
    line = lax.broadcasted_iota(jnp.int32, (16, HD), 0)
    for h in range(heads):
        peak = jnp.full((1, 1), -jnp.inf, jnp.float32)
        here = slice(h * HD, (h + 1) * HD)
        for g in range(groups):
            cols = []
            for r in range(ROLES):
                at = r * width + h * HD
                cols.append(jnp.concatenate([x[g, :, at : at + HD] for x in ins], axis=0))
            result, highest = attend(*cols, mask)
            peak = jnp.maximum(peak, highest * score_scale)
            result = result.astype(jnp.bfloat16)
            at = 0
            for out, pair in (place for spot in spots for place in spot):
                outs[out][g * 32 + pair * 16 : g * 32 + pair * 16 + 16, here] = result[at : at + 16]
                at += 16
        tail = jnp.zeros((16, HD), jnp.float32)
        both = pieces(peak_ref[0:1, here]) + pieces(jnp.broadcast_to(peak, (1, HD)))
        for i, value in enumerate(both):
            tail = jnp.where(line == i, value, tail)
        for out in outs:
            out[groups * 32 : groups * 32 + 16, here] = tail.astype(jnp.bfloat16)


def time_attention(parts, spots, peaks, heads, count):
    groups = parts[0].shape[0]
    width = heads * HD
    total = sum(16 * len(spot) for spot in spots)
    shape = jax.ShapeDtypeStruct((groups * 32 + 16, width), jnp.bfloat16)
    return pl.pallas_call(
        lambda *refs: time_kernel(heads, spots, *refs),
        in_specs=[VMEM] * (len(parts) + 1),
        out_specs=[VMEM] * count,
        out_shape=[shape] * count,
        compiler_params=PARAMS,
        cost_estimate=pl.CostEstimate(
            flops=4 * groups * heads * total * total * HD,
            bytes_accessed=8 * groups * total * width,
            transcendentals=groups * heads * total * total,
        ),
        name="time_attention",
    )(*parts, peaks)


def finish_kernel(direct, heads, index_ref, *refs):
    ins, out_ref, clip_ref = refs[:-2], refs[-2], refs[-1]
    groups = (ins[0].shape[0] - 16) // 32
    mine = index_ref[0]
    peak = None
    for d, source in enumerate(ins):
        for two in range(groups // 2):
            for pair in range(2):
                starts = [(2 * two + k) * 32 + pair * 16 for k in range(2)]
                a, b = (source[start : start + 16, :].astype(jnp.float32) for start in starts)
                for k in range(2):
                    tile = jnp.concatenate([a[8 * k : 8 * k + 8], b[8 * k : 8 * k + 8]], axis=0)
                    frame = 2 * pair + k if d in direct else mine ^ (2 * pair + k)
                    start = pl.multiple_of(index_ref[1 + d] * (groups * 8) + two * 16, 16)
                    out_ref[frame, pl.ds(start, 16), :] = tile.astype(jnp.bfloat16)
        tail = source[groups * 32 : groups * 32 + 16, :].astype(jnp.float32)
        values = [tail[3 * a : 3 * a + 1] + tail[3 * a + 1 : 3 * a + 2] + tail[3 * a + 2 : 3 * a + 3] for a in range(2)]
        peak = values if peak is None else [jnp.maximum(p, v) for p, v in zip(peak, values)]
    for a in range(2):
        clip_ref[a : a + 1, :] = jnp.sqrt(clip_limit / jnp.maximum(peak[a], clip_limit))


def finish(index, received, frames, positions, width, direct, heads):
    return pl.pallas_call(
        lambda *refs: finish_kernel(direct, heads, *refs),
        in_specs=[pl.BlockSpec(memory_space=pltpu.SMEM)] + [VMEM] * len(received),
        out_specs=[VMEM, VMEM],
        out_shape=[
            jax.ShapeDtypeStruct((frames, positions, width), jnp.bfloat16),
            jax.ShapeDtypeStruct((2, width), jnp.float32),
        ],
        compiler_params=PARAMS,
        name="finish",
    )(index, *received)


def swap(value, axis, size, distance):
    return lax.ppermute(value, axis, [(i, i ^ distance) for i in range(size)])


def fast_body(seq, head, patch_tokens, projection):
    frames, positions, depth = patch_tokens.shape
    heads = projection.shape[-1] // HD
    width = heads * HD
    rows = positions // seq
    me, mine = lax.axis_index("seq"), lax.axis_index("head")
    token_group, direct = (4, 5, 2, 3, 1), (0, 6, 7)
    owners = jnp.stack([me ^ d for d in range(seq)]).astype(jnp.int32)
    paired = jnp.transpose(projection, (0, 2, 1, 3))

    def piece(frame, owner):
        return lax.dynamic_slice(patch_tokens, (frame, owner * rows, 0), (1, rows, depth))

    got = [swap(piece(mine, me ^ d), "seq", seq, d) for d in token_group]
    index = jnp.stack([me ^ d for d in direct]).astype(jnp.int32)
    weights, own, *away = early(index, patch_tokens, paired, rows, len(direct))
    away = [swap(part, "seq", seq, d) for d, part in zip(direct[1:], away)]

    *got, weights = lax.optimization_barrier([*got, weights])
    here = jnp.concatenate(got, axis=0)
    there = swap(here, "head", head, 2)
    here_other = swap(here, "head", head, 1)
    parts, last, peaks = space_peak(patch_tokens, paired, heads)
    first = project(here, here_other, weights)
    there, peaks, first, *away = lax.optimization_barrier([there, peaks, first, *away])
    there_other = swap(there, "head", head, 1)
    second = project(there, there_other, weights)
    spots = [[(d, 0), (d, 1)] for d in direct] + [[(d, pair) for d in token_group] for pair in range(2)]
    outs = time_attention([own, *away, first, second], spots, peaks, heads, seq)
    *outs, parts = lax.optimization_barrier([*outs, parts])
    received = [out if d == 0 else swap(out, "seq", seq, d) for d, out in enumerate(outs)]
    space_out = space_attention(patch_tokens, last, parts, heads)
    finish_index = jnp.concatenate([mine.astype(jnp.int32)[None], owners])
    time_out, clip = finish(finish_index, received, frames, positions, width, direct, heads)
    return space_out, time_out, clip[:, ::HD]


def mixing(scores):
    highest = jnp.max(scores, axis=-1, keepdims=True)
    expon = jnp.exp(scores - highest)
    return (expon / jnp.sum(expon, axis=-1, keepdims=True)).astype(jnp.bfloat16)


def plain_attention(form, query_part, key_part, value_part):
    scores = jnp.einsum(form[0], query_part, key_part, preferred_element_type=jnp.float32) * score_scale
    result = jnp.einsum(form[1], mixing(scores), value_part, preferred_element_type=jnp.float32)
    return result.astype(jnp.bfloat16), jnp.max(scores, axis=(0, 2, 3))


def plain_body(patch_tokens, projection):
    frames, positions, depth = patch_tokens.shape
    heads = projection.shape[-1] // HD
    parts = jnp.dot(
        patch_tokens.reshape(-1, depth), projection.reshape(depth, -1), preferred_element_type=jnp.float32
    )
    parts = parts.astype(jnp.bfloat16).reshape(frames, positions, 2, ROLES, heads, HD)
    space_out, space_high = plain_attention(
        ("fihd,fjhd->fhij", "fhij,fjhd->fihd"), *(parts[:, :, 0, r] for r in range(ROLES))
    )
    moved = [lax.all_to_all(parts[:, :, 1, r], "seq", split_axis=1, concat_axis=0, tiled=True) for r in range(ROLES)]
    time_out, time_high = plain_attention(("fphd,gphd->phfg", "phfg,gphd->fphd"), *moved)
    time_out = lax.all_to_all(time_out, "seq", split_axis=0, concat_axis=1, tiled=True)
    peak = lax.pmax(jnp.stack([space_high, time_high]), "seq")
    clip_factor = jnp.sqrt(clip_limit / jnp.maximum(peak, clip_limit))
    flat = (frames, positions, heads * HD)
    return space_out.reshape(flat), time_out.reshape(flat), clip_factor


def solution(mesh):
    seq, head = mesh.shape["seq"], mesh.shape["head"]

    def body(patch_tokens, projection):
        frames, positions, _ = patch_tokens.shape
        if seq == 8 and head == 4 and frames == 4 and positions % (16 * seq) == 0:
            return fast_body(seq, head, patch_tokens, projection)
        return plain_body(patch_tokens, projection)

    return jax.shard_map(
        body,
        mesh=mesh,
        in_specs=(P("seq", None, None), P(None, None, None, "head")),
        out_specs=(P("seq", None, "head"), P("seq", None, "head"), P(None, "head")),
        check_vma=False,
    )
```

```python
import math

import jax
import jax.numpy as jnp
from jax import lax
from jax.experimental import pallas as pl
from jax.experimental.pallas import tpu as pltpu
from jax.sharding import PartitionSpec as P

HD = 128
ROLES = 3
clip_limit = 30.0
score_scale = 1.0 / math.sqrt(HD)
exp_scale = score_scale * math.log2(math.e)
VMEM = pl.BlockSpec(memory_space=pltpu.VMEM)
SMALL = pl.CostEstimate(flops=3000000000, bytes_accessed=8000000, transcendentals=0)
LARGE = pl.CostEstimate(flops=16000000000, bytes_accessed=40000000, transcendentals=0)
STEPS = 2
PARAMS = pltpu.CompilerParams(vmem_limit_bytes=48 * 1024 * 1024)


def dot_nt(a, b):
    return lax.dot_general(a, b, (((1,), (1,)), ((), ())), preferred_element_type=jnp.float32)


def attend(query_part, key_part, value_part, mask=None):
    raw = dot_nt(query_part, key_part)
    if mask is not None:
        raw = jnp.where(mask, raw, -jnp.inf)
    highest = jnp.max(raw, axis=-1, keepdims=True)
    expon = jnp.exp2((raw - highest) * exp_scale)
    weights = (expon * (1.0 / jnp.sum(expon, axis=-1, keepdims=True))).astype(jnp.bfloat16)
    result = jnp.dot(weights, value_part, preferred_element_type=jnp.float32)
    return result, jnp.max(highest, axis=0, keepdims=True)


def pick_matrix(which, chunk):
    rows = lax.broadcasted_iota(jnp.int32, (ROLES * chunk, ROLES * 2 * chunk), 0)
    cols = lax.broadcasted_iota(jnp.int32, (ROLES * chunk, ROLES * 2 * chunk), 1)
    source = ((rows % chunk) * ROLES + rows // chunk) * 2 + which
    return jnp.where(cols == source, 1.0, 0.0).astype(jnp.bfloat16)


def pick(pick_ref, w_ref, out_ref):
    depth, _, _, width = w_ref.shape
    chunk = pick_ref.shape[0] // ROLES
    span = 2 * ROLES * chunk
    flat = w_ref.reshape(depth * ROLES * 2, width)
    for i in range(depth // chunk):
        found = jnp.dot(pick_ref[...], flat[i * span : (i + 1) * span, :], preferred_element_type=jnp.float32)
        found = found.astype(jnp.bfloat16)
        for r in range(ROLES):
            out_ref[i * chunk : (i + 1) * chunk, r * width : (r + 1) * width] = found[r * chunk : (r + 1) * chunk]


def pair_rows(one, two, blocks, rows, store):
    for b in range(blocks):
        for g in range(rows // 8):
            at = b * rows + g * 8
            tile = jnp.concatenate([one[at : at + 8], two[at : at + 8]], axis=0)
            store(b, g, tile.astype(jnp.bfloat16))


def early_kernel(count, index_ref, *refs):
    xs, w_ref, weights_ref = refs[:count], refs[count], refs[count + 1]
    outs, (pick_ref, total) = refs[count + 2 : -2], refs[-2:]
    step = pl.program_id(0)

    @pl.when(step == 0)
    def _():
        pick_ref[...] = pick_matrix(1, CHUNK)
        total[...] = jnp.zeros_like(total)

    pick(pick_ref, w_ref, weights_ref)
    frames, rows, block = xs[0].shape
    tokens = jnp.concatenate([x[...].reshape(frames * rows, block) for x in xs], axis=0)
    total[...] += jnp.dot(tokens, weights_ref[...], preferred_element_type=jnp.float32)

    @pl.when(step == pl.num_programs(0) - 1)
    def _():
        for i, out in enumerate(outs):
            for pair in range(frames // 2):
                at = (i * frames + 2 * pair) * rows

                def store(b, g, tile):
                    out[g, pair * 16 : pair * 16 + 16, :] = tile

                pair_rows(total[at : at + rows], total[at + rows : at + 2 * rows], 1, rows, store)


CHUNK = 64


def early(index, tokens, paired, rows, count):
    frames, _, depth = tokens.shape
    width = paired.shape[-1]
    cols = ROLES * width
    block = 1024
    out = jax.ShapeDtypeStruct((rows // 8, frames * 8, cols), jnp.bfloat16)
    return pl.pallas_call(
        lambda *refs: early_kernel(count, *refs),
        grid_spec=pltpu.PrefetchScalarGridSpec(
            num_scalar_prefetch=1,
            grid=(depth // block,),
            in_specs=[
                pl.BlockSpec((frames, rows, block), lambda k, index, i=i: (0, index[i], k)) for i in range(count)
            ]
            + [pl.BlockSpec((block, ROLES, 2, width), lambda k, index: (k, 0, 0, 0))],
            out_specs=[pl.BlockSpec((block, cols), lambda k, index: (k, 0))]
            + [pl.BlockSpec(out.shape, lambda k, index: (0, 0, 0))] * count,
            scratch_shapes=[
                pltpu.VMEM((ROLES * CHUNK, 2 * ROLES * CHUNK), jnp.bfloat16),
                pltpu.VMEM((count * frames * rows, cols), jnp.float32),
            ],
        ),
        out_shape=[jax.ShapeDtypeStruct((depth, cols), jnp.bfloat16)] + [out] * count,
        compiler_params=PARAMS,
        cost_estimate=pl.CostEstimate(
            flops=2 * count * frames * rows * depth * cols + 12 * CHUNK * depth * cols,
            bytes_accessed=6 * depth * cols,
            transcendentals=0,
        ),
        name="early",
    )(index, *[tokens] * count, paired)


def space_peak_kernel(heads, x_ref, w_ref, parts_ref, last_ref, peak_ref, pick_ref, weights_ref, total):
    step = pl.program_id(0)
    frames, positions, block = x_ref.shape
    width = heads * HD

    @pl.when(step == 0)
    def _():
        pick_ref[...] = pick_matrix(0, CHUNK)
        total[...] = jnp.zeros_like(total)

    pick(pick_ref, w_ref, weights_ref)
    last_ref[...] = weights_ref[:, 2 * width :]
    tokens = x_ref[...].reshape(frames * positions, block)
    total[...] += jnp.dot(tokens, weights_ref[:, : 2 * width], preferred_element_type=jnp.float32)

    @pl.when(step == pl.num_programs(0) - 1)
    def _():
        parts_ref[...] = total[...].astype(jnp.bfloat16)
        for h in range(heads):
            peak = jnp.full((1, 1), -jnp.inf, jnp.float32)
            for f in range(frames):
                query_part, key_part = (
                    parts_ref[f * positions : (f + 1) * positions, r * width + h * HD : r * width + (h + 1) * HD]
                    for r in range(2)
                )
                peak = jnp.maximum(peak, jnp.max(dot_nt(query_part, key_part), keepdims=True))
            peak_ref[:, h * HD : (h + 1) * HD] = jnp.broadcast_to(peak * score_scale, (8, HD))


def space_peak(tokens, paired, heads):
    frames, positions, depth = tokens.shape
    width = heads * HD
    block = 512
    rows = frames * positions
    return pl.pallas_call(
        lambda *refs: space_peak_kernel(heads, *refs),
        grid=(depth // block,),
        in_specs=[
            pl.BlockSpec((frames, positions, block), lambda k: (0, 0, k)),
            pl.BlockSpec((block, ROLES, 2, width), lambda k: (k, 0, 0, 0)),
        ],
        out_specs=[
            pl.BlockSpec((rows, 2 * width), lambda k: (0, 0)),
            pl.BlockSpec((block, width), lambda k: (k, 0)),
            pl.BlockSpec((8, width), lambda k: (0, 0)),
        ],
        out_shape=[
            jax.ShapeDtypeStruct((rows, 2 * width), jnp.bfloat16),
            jax.ShapeDtypeStruct((depth, width), jnp.bfloat16),
            jax.ShapeDtypeStruct((8, width), jnp.float32),
        ],
        scratch_shapes=[
            pltpu.VMEM((ROLES * CHUNK, 2 * ROLES * CHUNK), jnp.bfloat16),
            pltpu.VMEM((block, ROLES * width), jnp.bfloat16),
            pltpu.VMEM((rows, 2 * width), jnp.float32),
        ],
        compiler_params=PARAMS,
        cost_estimate=SMALL,
        name="space_peak",
    )(tokens, paired)


def space_kernel(heads, x_ref, w_ref, parts_ref, out_ref):
    frames, positions, depth = x_ref.shape
    width = heads * HD
    tokens = x_ref[...].reshape(frames * positions, depth)
    values = jnp.dot(tokens, w_ref[...], preferred_element_type=jnp.float32).astype(jnp.bfloat16)
    for f in range(frames):
        rows = slice(f * positions, (f + 1) * positions)
        for h in range(heads):
            cols = [parts_ref[rows, r * width + h * HD : r * width + (h + 1) * HD] for r in range(2)]
            result, _ = attend(*cols, values[rows, h * HD : (h + 1) * HD])
            out_ref[f, :, h * HD : (h + 1) * HD] = result.astype(jnp.bfloat16)


def space_attention(tokens, weights, parts, heads):
    frames, positions, depth = tokens.shape
    width = heads * HD
    block = 2
    return pl.pallas_call(
        lambda *refs: space_kernel(heads, *refs),
        grid=(frames // block,),
        in_specs=[
            pl.BlockSpec((block, positions, depth), lambda f: (f, 0, 0)),
            pl.BlockSpec((depth, width), lambda f: (0, 0)),
            pl.BlockSpec((block * positions, 2 * width), lambda f: (f, 0)),
        ],
        out_specs=pl.BlockSpec((block, positions, width), lambda f: (f, 0, 0)),
        out_shape=jax.ShapeDtypeStruct((frames, positions, width), jnp.bfloat16),
        compiler_params=PARAMS,
        cost_estimate=LARGE,
        name="space_attention",
    )(tokens, weights, parts)


def pieces(value):
    high = value.astype(jnp.bfloat16).astype(jnp.float32)
    mid = (value - high).astype(jnp.bfloat16).astype(jnp.float32)
    return high, mid, value - high - mid


def pair_tiles(total, one, two, group):
    tile = jnp.concatenate([total[at + group * 8 : at + group * 8 + 8] for at in (one, two)], axis=0)
    return tile.astype(jnp.bfloat16)


def add_product(total, sources, w_ref):
    @pl.when(pl.program_id(0) == 0)
    def _():
        total[...] = jnp.zeros_like(total)

    tokens = jnp.concatenate([x[...].reshape(-1, x.shape[-1]) for x in sources], axis=0)
    total[...] += jnp.dot(tokens, w_ref[...], preferred_element_type=jnp.float32)


def project_kernel(index_ref, one_ref, two_ref, own_ref, w_ref, out_ref, total):
    blocks, rows, _ = one_ref.shape
    frames = own_ref.shape[0]
    add_product(total, (one_ref, two_ref, own_ref), w_ref)

    @pl.when(pl.program_id(0) == pl.num_programs(0) - 1)
    def _():
        pairs = [(b, blocks + b) for b in range(blocks)]
        pairs += [(2 * blocks + f, 2 * blocks + f + 1) for f in range(0, frames, 2)]
        for g in range(rows // 8):
            for i, (one, two) in enumerate(pairs):
                out_ref[g, i * 16 : i * 16 + 16, :] = pair_tiles(total, one * rows, two * rows, g)


def project(index, one, two, tokens, weights):
    blocks, rows, depth = one.shape
    frames = tokens.shape[0]
    cols = weights.shape[1]
    block = depth // STEPS
    here = (2 * blocks + frames) * rows
    shape = (rows // 8, (2 * blocks + frames) * 8, cols)
    return pl.pallas_call(
        project_kernel,
        grid_spec=pltpu.PrefetchScalarGridSpec(
            num_scalar_prefetch=1,
            grid=(STEPS,),
            in_specs=[pl.BlockSpec((blocks, rows, block), lambda k, index: (0, 0, k))] * 2
            + [
                pl.BlockSpec((frames, rows, block), lambda k, index: (0, index[0], k)),
                pl.BlockSpec((block, cols), lambda k, index: (k, 0)),
            ],
            out_specs=pl.BlockSpec(shape, lambda k, index: (0, 0, 0)),
            scratch_shapes=[pltpu.VMEM((here, cols), jnp.float32)],
        ),
        out_shape=jax.ShapeDtypeStruct(shape, jnp.bfloat16),
        compiler_params=PARAMS,
        cost_estimate=LARGE,
        name="project",
    )(index, one, two, tokens, weights)


def late_kernel(heads, spots, blocks_to, *refs):
    (one_ref, two_ref, w_ref), ins, peak_ref = refs[:3], refs[3 : 3 + len(spots)], refs[3 + len(spots)]
    outs, (total, parts_ref) = refs[4 + len(spots) : -2], refs[-2:]
    blocks, rows, _ = one_ref.shape
    add_product(total, (one_ref, two_ref), w_ref)

    @pl.when(pl.program_id(0) == pl.num_programs(0) - 1)
    def _():
        for b in range(blocks):
            for g in range(rows // 8):
                parts_ref[g, b * 16 : b * 16 + 16, :] = pair_tiles(total, b * rows, (blocks + b) * rows, g)
        places = [place for spot in spots for place in spot] + [(d, 1) for d in blocks_to]
        attend_time(heads, places, [*ins, parts_ref], peak_ref, outs)


def attend_time(heads, spots, ins, peak_ref, outs):
    groups = ins[0].shape[0]
    width = heads * HD
    size = 16 * len(spots)
    row = lax.broadcasted_iota(jnp.int32, (size, size), 0)
    col = lax.broadcasted_iota(jnp.int32, (size, size), 1)
    mask = ((row ^ col) & 7) == 0
    line = lax.broadcasted_iota(jnp.int32, (16, HD), 0)
    lane = lax.broadcasted_iota(jnp.int32, (16, HD), 1) // TAIL
    tail = jnp.zeros((16, HD), jnp.float32)
    for h in range(heads):
        peak = jnp.full((1, 1), -jnp.inf, jnp.float32)
        for g in range(groups):
            cols = []
            for r in range(ROLES):
                at = r * width + h * HD
                cols.append(jnp.concatenate([x[g, :, at : at + HD] for x in ins], axis=0))
            result, highest = attend(*cols, mask)
            peak = jnp.maximum(peak, highest * score_scale)
            result = result.astype(jnp.bfloat16)
            for i, (out, pair) in enumerate(spots):
                start = (h * groups + g) * 32 + pair * 16
                outs[out][start : start + 16, :] = result[i * 16 : i * 16 + 16]
        both = pieces(peak_ref[0:1, h * HD : (h + 1) * HD]) + pieces(jnp.broadcast_to(peak, (1, HD)))
        for i, value in enumerate(both):
            tail = jnp.where((line == i) & (lane == h), value, tail)
    for out in outs:
        out[heads * groups * 32 :, :] = tail.astype(jnp.bfloat16)


TAIL = 32


def late(one, two, weights, parts, spots, peaks, heads, count, blocks_to):
    blocks, rows, depth = one.shape
    cols = weights.shape[1]
    groups = rows // 8
    block = depth // STEPS
    shape = (heads * groups * 32 + 16, HD)

    def whole(shape):
        return pl.BlockSpec(shape, lambda k: (0,) * len(shape))

    return pl.pallas_call(
        lambda *refs: late_kernel(heads, spots, blocks_to, *refs),
        grid=(STEPS,),
        in_specs=[pl.BlockSpec((blocks, rows, block), lambda k: (0, 0, k))] * 2
        + [pl.BlockSpec((block, cols), lambda k: (k, 0))]
        + [whole(part.shape) for part in (*parts, peaks)],
        out_specs=[whole(shape)] * count,
        out_shape=[jax.ShapeDtypeStruct(shape, jnp.bfloat16)] * count,
        scratch_shapes=[
            pltpu.VMEM((2 * blocks * rows, cols), jnp.float32),
            pltpu.VMEM((groups, blocks * 16, cols), jnp.bfloat16),
        ],
        compiler_params=PARAMS,
        cost_estimate=LARGE,
        name="late",
    )(one, two, weights, *parts, peaks)


def finish_kernel(direct, heads, index_ref, *refs):
    ins, out_ref, clip_ref = refs[:-2], refs[-2], refs[-1]
    groups = (ins[0].shape[0] - 16) // (32 * heads)
    mine = index_ref[0]
    peak = None
    for d, source in enumerate(ins):
        for h in range(heads):
            for two in range(groups // 2):
                for pair in range(2):
                    starts = [(h * groups + 2 * two + k) * 32 + pair * 16 for k in range(2)]
                    a, b = (source[start : start + 16, :].astype(jnp.float32) for start in starts)
                    for k in range(2):
                        tile = jnp.concatenate([a[8 * k : 8 * k + 8], b[8 * k : 8 * k + 8]], axis=0)
                        frame = 2 * pair + k if d in direct else mine ^ (pair + 2 * k)
                        start = pl.multiple_of(index_ref[1 + d] * (groups * 8) + two * 16, 16)
                        out_ref[frame, pl.ds(start, 16), h * HD : (h + 1) * HD] = tile.astype(jnp.bfloat16)
        tail = source[heads * groups * 32 :, :].astype(jnp.float32)
        values = [tail[3 * a : 3 * a + 1] + tail[3 * a + 1 : 3 * a + 2] + tail[3 * a + 2 : 3 * a + 3] for a in range(2)]
        peak = values if peak is None else [jnp.maximum(p, v) for p, v in zip(peak, values)]
    for a in range(2):
        clip = jnp.sqrt(clip_limit / jnp.maximum(peak[a], clip_limit))
        clip_ref[a : a + 1, :] = jnp.concatenate([clip[:, h * TAIL : h * TAIL + 1] for h in range(heads)], axis=1)


def finish(index, received, frames, positions, direct, heads):
    return pl.pallas_call(
        lambda *refs: finish_kernel(direct, heads, *refs),
        in_specs=[pl.BlockSpec(memory_space=pltpu.SMEM)] + [VMEM] * len(received),
        out_specs=[VMEM, VMEM],
        out_shape=[
            jax.ShapeDtypeStruct((frames, positions, heads * HD), jnp.bfloat16),
            jax.ShapeDtypeStruct((2, heads), jnp.float32),
        ],
        compiler_params=PARAMS,
        name="finish",
    )(index, *received)


def swap(value, axis, size, distance):
    return lax.ppermute(value, axis, [(i, i ^ distance) for i in range(size)])


def fast_body(seq, head, patch_tokens, projection):
    frames, positions, depth = patch_tokens.shape
    heads = projection.shape[-1] // HD
    width = heads * HD
    rows = positions // seq
    me, mine = lax.axis_index("seq"), lax.axis_index("head")
    token_group, direct = (3, 2, 5, 4), (6, 7, 1)
    paired = jnp.transpose(projection, (0, 2, 1, 3))

    def piece(frame, owner):
        return lax.dynamic_slice(patch_tokens, (frame, owner * rows, 0), (1, rows, depth))

    got = [swap(piece(mine, me ^ d), "seq", seq, d) for d in token_group]
    index = jnp.stack([me ^ d for d in direct]).astype(jnp.int32)
    weights, *away = early(index, patch_tokens, paired, rows, len(direct))
    away = [swap(part, "seq", seq, d) for d, part in zip(direct, away)]

    *got, weights = lax.optimization_barrier([*got, weights])
    here = jnp.concatenate(got, axis=0)
    there = swap(here, "head", head, 2)
    parts, last, peaks = space_peak(patch_tokens, paired, heads)
    here, there, peaks = lax.optimization_barrier([here, there, peaks])
    here_other = swap(here, "head", head, 1)
    there_other = swap(there, "head", head, 1)
    first = project(me.astype(jnp.int32)[None], here, there, patch_tokens, weights)
    spots = [[(d, 0), (d, 1)] for d in direct] + [[(d, 0) for d in token_group] + [(0, 0), (0, 1)]]
    outs = late(here_other, there_other, weights, [*away, first], spots, peaks, heads, seq, token_group)
    *outs, parts = lax.optimization_barrier([*outs, parts])
    order = (0, 1, 2, 4, 5, 6, 7, 3)
    received = [outs[d] if d == 0 else swap(outs[d], "seq", seq, d) for d in order]
    space_out = space_attention(patch_tokens, last, parts, heads)
    finish_index = jnp.stack([mine] + [me ^ d for d in order]).astype(jnp.int32)
    natural = [i for i, d in enumerate(order) if d not in token_group]
    time_out, clip = finish(finish_index, received, frames, positions, natural, heads)
    return space_out, time_out, clip


def mixing(scores):
    highest = jnp.max(scores, axis=-1, keepdims=True)
    expon = jnp.exp(scores - highest)
    return (expon / jnp.sum(expon, axis=-1, keepdims=True)).astype(jnp.bfloat16)


def plain_attention(form, query_part, key_part, value_part):
    scores = jnp.einsum(form[0], query_part, key_part, preferred_element_type=jnp.float32) * score_scale
    result = jnp.einsum(form[1], mixing(scores), value_part, preferred_element_type=jnp.float32)
    return result.astype(jnp.bfloat16), jnp.max(scores, axis=(0, 2, 3))


def plain_body(patch_tokens, projection):
    frames, positions, depth = patch_tokens.shape
    heads = projection.shape[-1] // HD
    parts = jnp.dot(
        patch_tokens.reshape(-1, depth), projection.reshape(depth, -1), preferred_element_type=jnp.float32
    )
    parts = parts.astype(jnp.bfloat16).reshape(frames, positions, 2, ROLES, heads, HD)
    space_out, space_high = plain_attention(
        ("fihd,fjhd->fhij", "fhij,fjhd->fihd"), *(parts[:, :, 0, r] for r in range(ROLES))
    )
    moved = [lax.all_to_all(parts[:, :, 1, r], "seq", split_axis=1, concat_axis=0, tiled=True) for r in range(ROLES)]
    time_out, time_high = plain_attention(("fphd,gphd->phfg", "phfg,gphd->fphd"), *moved)
    time_out = lax.all_to_all(time_out, "seq", split_axis=0, concat_axis=1, tiled=True)
    peak = lax.pmax(jnp.stack([space_high, time_high]), "seq")
    clip_factor = jnp.sqrt(clip_limit / jnp.maximum(peak, clip_limit))
    flat = (frames, positions, heads * HD)
    return space_out.reshape(flat), time_out.reshape(flat), clip_factor


def solution(mesh):
    seq, head = mesh.shape["seq"], mesh.shape["head"]

    def body(patch_tokens, projection):
        frames, positions, _ = patch_tokens.shape
        if seq == 8 and head == 4 and frames == 4 and positions % (16 * seq) == 0 and projection.shape[-1] <= 4 * HD:
            return fast_body(seq, head, patch_tokens, projection)
        return plain_body(patch_tokens, projection)

    return jax.shard_map(
        body,
        mesh=mesh,
        in_specs=(P("seq", None, None), P(None, None, None, "head")),
        out_specs=(P("seq", None, "head"), P("seq", None, "head"), P(None, "head")),
        check_vma=False,
    )
```

```python
import math

import jax
import jax.numpy as jnp
from jax import lax
from jax.experimental import pallas as pl
from jax.experimental.pallas import tpu as pltpu
from jax.sharding import PartitionSpec as P

HD = 128
ROLES = 3
clip_limit = 30.0
score_scale = 1.0 / math.sqrt(HD)
exp_scale = score_scale * math.log2(math.e)
VMEM = pl.BlockSpec(memory_space=pltpu.VMEM)
SMALL = pl.CostEstimate(flops=3000000000, bytes_accessed=8000000, transcendentals=0)
LARGE = pl.CostEstimate(flops=16000000000, bytes_accessed=40000000, transcendentals=0)
PARAMS = pltpu.CompilerParams(vmem_limit_bytes=32 * 1024 * 1024)


def in_hbm(value):
    return pltpu.with_memory_space_constraint(value, pltpu.HBM)


def dot_nt(a, b):
    return lax.dot_general(a, b, (((1,), (1,)), ((), ())), preferred_element_type=jnp.float32)


def attend(query_part, key_part, value_part, mask=None):
    raw = dot_nt(query_part, key_part)
    if mask is not None:
        raw = jnp.where(mask, raw, -jnp.inf)
    highest = jnp.max(raw, axis=-1, keepdims=True)
    expon = jnp.exp2((raw - highest) * exp_scale)
    weights = (expon * (1.0 / jnp.sum(expon, axis=-1, keepdims=True))).astype(jnp.bfloat16)
    result = jnp.dot(weights, value_part, preferred_element_type=jnp.float32)
    return result, jnp.max(highest, axis=0, keepdims=True)


def pick_matrix(which, chunk):
    rows = lax.broadcasted_iota(jnp.int32, (ROLES * chunk, ROLES * 2 * chunk), 0)
    cols = lax.broadcasted_iota(jnp.int32, (ROLES * chunk, ROLES * 2 * chunk), 1)
    source = ((rows % chunk) * ROLES + rows // chunk) * 2 + which
    return jnp.where(cols == source, 1.0, 0.0).astype(jnp.bfloat16)


def pick(pick_ref, w_ref, out_refs):
    depth, _, _, width = w_ref.shape
    chunk = pick_ref.shape[0] // ROLES
    span = 2 * ROLES * chunk
    flat = w_ref.reshape(depth * ROLES * 2, width)
    for i in range(depth // chunk):
        found = jnp.dot(pick_ref[...], flat[i * span : (i + 1) * span, :], preferred_element_type=jnp.float32)
        found = found.astype(jnp.bfloat16)
        for r in range(ROLES):
            out_refs[r][i * chunk : (i + 1) * chunk, :] = found[r * chunk : (r + 1) * chunk]


CHUNK = 64


def early_kernel(count, rows, index_ref, tokens_ref, w_ref, out_weights_ref, flag_ref, *refs):
    outs, (held, weights_ref, pick_ref, x_ref, w_sems, out_sems, x_sems) = refs[:count], refs[count:]
    frames, _, depth = tokens_ref.shape
    block = held.shape[1]
    steps = depth // block

    def load(step):
        return pltpu.make_async_copy(w_ref.at[pl.ds(step * block, block)], held.at[step % SLOTS], w_sems.at[step % SLOTS])

    def store(step):
        here = pl.ds(step * block, block)
        return pltpu.make_async_copy(weights_ref.at[here], out_weights_ref.at[here], out_sems.at[step])

    for step in range(SLOTS - 1):
        load(step).start()
    loads = []
    for i in range(count):
        start = pl.multiple_of(index_ref[i] * rows, rows)
        for f in range(frames):
            at = i * frames + f
            loads.append(
                pltpu.make_async_copy(
                    tokens_ref.at[f, pl.ds(start, rows)], x_ref.at[pl.ds(at * rows, rows)], x_sems.at[at]
                )
            )
            loads[-1].start()
    pick_ref[...] = pick_matrix(1, CHUNK)
    for step in range(steps):
        if step + SLOTS - 1 < steps:
            load(step + SLOTS - 1).start()
        load(step).wait()
        here = pl.ds(step * block, block)
        width = held.shape[-1]
        outs_at = [weights_ref.at[here, r * width : (r + 1) * width] for r in range(ROLES)]
        pick(pick_ref, held.at[step % SLOTS], outs_at)
        store(step).start()
    for copy in loads:
        copy.wait()
    total = jnp.dot(x_ref[...], weights_ref[...], preferred_element_type=jnp.float32)
    flag_ref[...] = jnp.zeros_like(flag_ref)
    for i, out in enumerate(outs):
        for pair in range(frames // 2):
            at = (i * frames + 2 * pair) * rows
            for g in range(rows // 8):
                out[g, pair * 16 : pair * 16 + 16, :] = pair_tiles(total, at, at + rows, g)
    for step in range(steps):
        store(step).wait()


def early(index, tokens, paired, rows, count):
    frames, _, depth = tokens.shape
    width = paired.shape[-1]
    cols = ROLES * width
    block = BLOCK
    out = jax.ShapeDtypeStruct((rows // 8, frames * 8, cols), jnp.bfloat16)
    here = count * frames * rows
    return pl.pallas_call(
        lambda *refs: early_kernel(count, rows, *refs),
        in_specs=[pl.BlockSpec(memory_space=pltpu.SMEM)] + [pl.BlockSpec(memory_space=pl.ANY)] * 2,
        out_specs=[pl.BlockSpec(memory_space=pl.ANY)] + [VMEM] * (1 + count),
        out_shape=[pltpu.HBM((depth, cols), jnp.bfloat16), jax.ShapeDtypeStruct((8, HD), jnp.float32)] + [out] * count,
        scratch_shapes=[
            pltpu.VMEM((SLOTS, block, ROLES, 2, width), jnp.bfloat16),
            pltpu.VMEM((depth, cols), jnp.bfloat16),
            pltpu.VMEM((ROLES * CHUNK, 2 * ROLES * CHUNK), jnp.bfloat16),
            pltpu.VMEM((here, depth), jnp.bfloat16),
            pltpu.SemaphoreType.DMA((SLOTS,)),
            pltpu.SemaphoreType.DMA((depth // block,)),
            pltpu.SemaphoreType.DMA((count * frames,)),
        ],
        compiler_params=PARAMS,
        cost_estimate=LARGE,
        name="early",
    )(index, in_hbm(tokens), in_hbm(paired))


BLOCK = 512
SLOTS = 3
SPLITS = 3


def space_peak_kernel(heads, x_hbm, w_hbm, flag_ref, parts_hbm, last_hbm, peak_ref, *scratch):
    held, x_ref, weights_ref, last_ref, parts_ref, pick_ref, w_sems, x_sem, last_sem, parts_sem = scratch
    frames, positions, depth = x_hbm.shape
    steps, block = held.shape[:2]
    width = heads * HD
    loads = [pltpu.make_async_copy(w_hbm.at[pl.ds(i * block, block)], held.at[i], w_sems.at[i]) for i in range(steps)]
    for load in loads:
        load.start()
    load_tokens = pltpu.make_async_copy(x_hbm, x_ref, x_sem.at[0])
    load_tokens.start()
    pick_ref[...] = pick_matrix(0, CHUNK)
    for step in range(steps):
        loads[step].wait()
        here = pl.ds(step * block, block)
        outs = [weights_ref.at[here, r * width : (r + 1) * width] for r in range(2)] + [last_ref.at[here]]
        pick(pick_ref, held.at[step], outs)
    store_last = pltpu.make_async_copy(last_ref, last_hbm, last_sem.at[0])
    store_last.start()
    load_tokens.wait()
    tokens = x_ref[...].reshape(frames * positions, depth)
    parts_ref[...] = jnp.dot(tokens, weights_ref[...], preferred_element_type=jnp.float32).astype(jnp.bfloat16)
    store = pltpu.make_async_copy(parts_ref, parts_hbm, parts_sem.at[0])
    store.start()
    for h in range(heads):
        peak = jnp.full((1, 1), -jnp.inf, jnp.float32)
        for f in range(frames):
            query_part, key_part = (
                parts_ref[f * positions : (f + 1) * positions, r * width + h * HD : r * width + (h + 1) * HD]
                for r in range(2)
            )
            peak = jnp.maximum(peak, jnp.max(dot_nt(query_part, key_part), keepdims=True))
        peak_ref[:, h * HD : (h + 1) * HD] = jnp.broadcast_to(peak * score_scale, (8, HD))
    store.wait()
    store_last.wait()


def space_peak(tokens, paired, flag, heads):
    frames, positions, depth = tokens.shape
    width = heads * HD
    rows = frames * positions
    block = BLOCK
    place = pl.BlockSpec(memory_space=pl.ANY)
    return pl.pallas_call(
        lambda *refs: space_peak_kernel(heads, *refs),
        in_specs=[place] * 3,
        out_specs=[place, place, VMEM],
        out_shape=[
            pltpu.HBM((rows, 2 * width), jnp.bfloat16),
            pltpu.HBM((depth, width), jnp.bfloat16),
            jax.ShapeDtypeStruct((8, width), jnp.float32),
        ],
        scratch_shapes=[
            pltpu.VMEM((depth // block, block, ROLES, 2, width), jnp.bfloat16),
            pltpu.VMEM(tokens.shape, jnp.bfloat16),
            pltpu.VMEM((depth, 2 * width), jnp.bfloat16),
            pltpu.VMEM((depth, width), jnp.bfloat16),
            pltpu.VMEM((rows, 2 * width), jnp.bfloat16),
            pltpu.VMEM((ROLES * CHUNK, 2 * ROLES * CHUNK), jnp.bfloat16),
            pltpu.SemaphoreType.DMA((depth // block,)),
            pltpu.SemaphoreType.DMA((1,)),
            pltpu.SemaphoreType.DMA((1,)),
            pltpu.SemaphoreType.DMA((1,)),
        ],
        compiler_params=pltpu.CompilerParams(vmem_limit_bytes=46 * 1024 * 1024),
        cost_estimate=SMALL,
        name="space_peak",
    )(in_hbm(tokens), in_hbm(paired), flag)


def space_kernel(heads, x_hbm, w_hbm, parts_hbm, out_hbm, x_ref, w_ref, parts_ref, out_ref, total, x_sems, w_sems, parts_sem, out_sems):
    frames, positions, depth = x_hbm.shape
    width = heads * HD
    span = depth // SPLITS
    loads = []
    for split in range(SPLITS):
        here = pl.ds(split * span, span)
        loads.append(
            (
                pltpu.make_async_copy(w_hbm.at[here], w_ref.at[here], w_sems.at[split]),
                pltpu.make_async_copy(x_hbm.at[:, :, here], x_ref.at[:, :, here], x_sems.at[split]),
            )
        )
    loads.append([pltpu.make_async_copy(parts_hbm, parts_ref, parts_sem.at[0])])
    for group in loads:
        for copy in group:
            copy.start()
    for split in range(SPLITS):
        for copy in loads[split]:
            copy.wait()
        at = split * span
        tokens = x_ref[:, :, at : at + span].reshape(frames * positions, span)
        part = jnp.dot(tokens, w_ref[at : at + span, :], preferred_element_type=jnp.float32)
        total[...] = part if split == 0 else total[...] + part
    loads[-1][0].wait()
    stores = []
    for f in range(frames):
        rows = slice(f * positions, (f + 1) * positions)
        for h in range(heads):
            cols = [parts_ref[rows, r * width + h * HD : r * width + (h + 1) * HD] for r in range(2)]
            result, _ = attend(*cols, total[rows, h * HD : (h + 1) * HD].astype(jnp.bfloat16))
            out_ref[f, :, h * HD : (h + 1) * HD] = result.astype(jnp.bfloat16)
        stores.append(pltpu.make_async_copy(out_ref.at[f], out_hbm.at[f], out_sems.at[f]))
        stores[-1].start()
    for store in stores:
        store.wait()


def space_attention(tokens, weights, parts, heads):
    frames, positions, depth = tokens.shape
    width = heads * HD
    rows = frames * positions
    place = pl.BlockSpec(memory_space=pl.ANY)
    return pl.pallas_call(
        lambda *refs: space_kernel(heads, *refs),
        in_specs=[place] * 3,
        out_specs=place,
        out_shape=jax.ShapeDtypeStruct((frames, positions, width), jnp.bfloat16),
        scratch_shapes=[
            pltpu.VMEM(tokens.shape, jnp.bfloat16),
            pltpu.VMEM((depth, width), jnp.bfloat16),
            pltpu.VMEM((rows, 2 * width), jnp.bfloat16),
            pltpu.VMEM((frames, positions, width), jnp.bfloat16),
            pltpu.VMEM((rows, width), jnp.float32),
            pltpu.SemaphoreType.DMA((SPLITS,)),
            pltpu.SemaphoreType.DMA((SPLITS,)),
            pltpu.SemaphoreType.DMA((1,)),
            pltpu.SemaphoreType.DMA((frames,)),
        ],
        compiler_params=PARAMS,
        cost_estimate=LARGE,
        name="space_attention",
    )(in_hbm(tokens), in_hbm(weights), in_hbm(parts))


def pieces(value):
    high = value.astype(jnp.bfloat16).astype(jnp.float32)
    mid = (value - high).astype(jnp.bfloat16).astype(jnp.float32)
    return high, mid, value - high - mid


def pair_tiles(total, one, two, group):
    tile = jnp.concatenate([total[at + group * 8 : at + group * 8 + 8] for at in (one, two)], axis=0)
    return tile.astype(jnp.bfloat16)


def project_kernel(blocks, rows, one_ref, two_ref, w_ref, out_ref):
    tokens = jnp.concatenate([one_ref[...], two_ref[...]], axis=0)
    total = jnp.dot(tokens, w_ref[...], preferred_element_type=jnp.float32)
    for g in range(rows // 8):
        for b in range(blocks):
            out_ref[g, b * 16 : b * 16 + 16, :] = pair_tiles(total, b * rows, (blocks + b) * rows, g)


def project(one, two, weights):
    blocks, rows, depth = one.shape
    return pl.pallas_call(
        lambda *refs: project_kernel(blocks, rows, *refs),
        in_specs=[VMEM] * 3,
        out_specs=VMEM,
        out_shape=jax.ShapeDtypeStruct((rows // 8, blocks * 16, weights.shape[1]), jnp.bfloat16),
        compiler_params=PARAMS,
        cost_estimate=LARGE,
        name="project",
    )(*[x.reshape(-1, depth) for x in (one, two)], pltpu.with_memory_space_constraint(weights, pltpu.VMEM))


def late_kernel(heads, spots, blocks_to, rows, *refs):
    (one_ref, two_ref, w_ref), ins, peak_ref = refs[:3], refs[3 : 3 + len(spots)], refs[3 + len(spots)]
    outs, parts_ref = refs[4 + len(spots) : -1], refs[-1]
    blocks = len(blocks_to)
    tokens = jnp.concatenate([one_ref[...], two_ref[...]], axis=0)
    total = jnp.dot(tokens, w_ref[...], preferred_element_type=jnp.float32)
    for b in range(blocks):
        for g in range(rows // 8):
            parts_ref[g, b * 16 : b * 16 + 16, :] = pair_tiles(total, b * rows, (blocks + b) * rows, g)
    places = [place for spot in spots for place in spot] + [(d, 1) for d in blocks_to]
    attend_time(heads, places, [*ins, parts_ref], peak_ref, outs)


def attend_time(heads, spots, ins, peak_ref, outs):
    groups = ins[0].shape[0]
    width = heads * HD
    size = 16 * len(spots)
    row = lax.broadcasted_iota(jnp.int32, (size, size), 0)
    col = lax.broadcasted_iota(jnp.int32, (size, size), 1)
    mask = ((row ^ col) & 7) == 0
    line = lax.broadcasted_iota(jnp.int32, (16, HD), 0)
    lane = lax.broadcasted_iota(jnp.int32, (16, HD), 1) // TAIL
    tail = jnp.zeros((16, HD), jnp.float32)
    for h in range(heads):
        peak = jnp.full((1, 1), -jnp.inf, jnp.float32)
        for g in range(groups):
            cols = []
            for r in range(ROLES):
                at = r * width + h * HD
                cols.append(jnp.concatenate([x[g, :, at : at + HD] for x in ins], axis=0))
            result, highest = attend(*cols, mask)
            peak = jnp.maximum(peak, highest * score_scale)
            result = result.astype(jnp.bfloat16)
            for i, (out, pair) in enumerate(spots):
                start = (h * groups + g) * 32 + pair * 16
                outs[out][start : start + 16, :] = result[i * 16 : i * 16 + 16]
        both = pieces(peak_ref[0:1, h * HD : (h + 1) * HD]) + pieces(jnp.broadcast_to(peak, (1, HD)))
        for i, value in enumerate(both):
            tail = jnp.where((line == i) & (lane == h), value, tail)
    for out in outs:
        out[heads * groups * 32 :, :] = tail.astype(jnp.bfloat16)


TAIL = 32


def late(one, two, weights, parts, spots, peaks, heads, count, blocks_to):
    blocks, rows, depth = one.shape
    cols = weights.shape[1]
    groups = rows // 8
    shape = (heads * groups * 32 + 16, HD)
    return pl.pallas_call(
        lambda *refs: late_kernel(heads, spots, blocks_to, rows, *refs),
        in_specs=[VMEM] * (4 + len(parts)),
        out_specs=[VMEM] * count,
        out_shape=[jax.ShapeDtypeStruct(shape, jnp.bfloat16)] * count,
        scratch_shapes=[
            pltpu.VMEM((groups, blocks * 16, cols), jnp.bfloat16),
        ],
        compiler_params=PARAMS,
        cost_estimate=LARGE,
        name="late",
    )(
        *[x.reshape(-1, depth) for x in (one, two)],
        pltpu.with_memory_space_constraint(weights, pltpu.VMEM),
        *parts,
        peaks,
    )


def finish_kernel(direct, heads, index_ref, *refs):
    ins, out_ref, clip_ref = refs[:-2], refs[-2], refs[-1]
    groups = (ins[0].shape[0] - 16) // (32 * heads)
    mine = index_ref[0]
    peak = None
    for d, source in enumerate(ins):
        for h in range(heads):
            for two in range(groups // 2):
                for pair in range(2):
                    starts = [(h * groups + 2 * two + k) * 32 + pair * 16 for k in range(2)]
                    a, b = (source[start : start + 16, :].astype(jnp.float32) for start in starts)
                    for k in range(2):
                        tile = jnp.concatenate([a[8 * k : 8 * k + 8], b[8 * k : 8 * k + 8]], axis=0)
                        frame = 2 * pair + k if d in direct else mine ^ (pair + 2 * k)
                        start = pl.multiple_of(index_ref[1 + d] * (groups * 8) + two * 16, 16)
                        out_ref[frame, pl.ds(start, 16), h * HD : (h + 1) * HD] = tile.astype(jnp.bfloat16)
        tail = source[heads * groups * 32 :, :].astype(jnp.float32)
        values = [tail[3 * a : 3 * a + 1] + tail[3 * a + 1 : 3 * a + 2] + tail[3 * a + 2 : 3 * a + 3] for a in range(2)]
        peak = values if peak is None else [jnp.maximum(p, v) for p, v in zip(peak, values)]
    for a in range(2):
        clip = jnp.sqrt(clip_limit / jnp.maximum(peak[a], clip_limit))
        clip_ref[a : a + 1, :] = jnp.concatenate([clip[:, h * TAIL : h * TAIL + 1] for h in range(heads)], axis=1)


def finish(index, received, frames, positions, direct, heads):
    return pl.pallas_call(
        lambda *refs: finish_kernel(direct, heads, *refs),
        in_specs=[pl.BlockSpec(memory_space=pltpu.SMEM)] + [VMEM] * len(received),
        out_specs=[VMEM, VMEM],
        out_shape=[
            jax.ShapeDtypeStruct((frames, positions, heads * HD), jnp.bfloat16),
            jax.ShapeDtypeStruct((2, heads), jnp.float32),
        ],
        compiler_params=PARAMS,
        name="finish",
    )(index, *received)


def swap(value, axis, size, distance):
    return lax.ppermute(value, axis, [(i, i ^ distance) for i in range(size)])


def fast_body(seq, head, patch_tokens, projection):
    frames, positions, depth = patch_tokens.shape
    heads = projection.shape[-1] // HD
    width = heads * HD
    rows = positions // seq
    me, mine = lax.axis_index("seq"), lax.axis_index("head")
    token_group, direct = (3, 2, 5, 4), (6, 7, 1)
    paired = jnp.transpose(projection, (0, 2, 1, 3))

    def piece(frame, owner):
        return lax.dynamic_slice(patch_tokens, (frame, owner * rows, 0), (1, rows, depth))

    got = [swap(piece(mine, me ^ d), "seq", seq, d) for d in token_group]
    index = jnp.stack([me ^ d for d in (*direct, 0)]).astype(jnp.int32)
    weights, flag, *away, own = early(index, patch_tokens, paired, rows, len(direct) + 1)
    away = [swap(part, "seq", seq, d) for d, part in zip(direct, away)]

    *got, flag = lax.optimization_barrier([*got, flag])
    here = jnp.concatenate(got, axis=0)
    there = swap(here, "head", head, 2)
    parts, last, peaks = space_peak(patch_tokens, paired, flag, heads)
    here, there, peaks = lax.optimization_barrier([here, there, peaks])
    here_other = swap(here, "head", head, 1)
    there_other = swap(there, "head", head, 1)
    first = project(here, there, weights)
    spots = [[(d, 0), (d, 1)] for d in (*direct, 0)] + [[(d, 0) for d in token_group]]
    outs = late(here_other, there_other, weights, [*away, own, first], spots, peaks, heads, seq, token_group)
    *outs, parts = lax.optimization_barrier([*outs, parts])
    order = (0, 1, 2, 4, 5, 6, 7, 3)
    received = [outs[d] if d == 0 else swap(outs[d], "seq", seq, d) for d in order]
    space_out = space_attention(patch_tokens, last, parts, heads)
    finish_index = jnp.stack([mine] + [me ^ d for d in order]).astype(jnp.int32)
    natural = [i for i, d in enumerate(order) if d not in token_group]
    time_out, clip = finish(finish_index, received, frames, positions, natural, heads)
    return space_out, time_out, clip


def mixing(scores):
    highest = jnp.max(scores, axis=-1, keepdims=True)
    expon = jnp.exp(scores - highest)
    return (expon / jnp.sum(expon, axis=-1, keepdims=True)).astype(jnp.bfloat16)


def plain_attention(form, query_part, key_part, value_part):
    scores = jnp.einsum(form[0], query_part, key_part, preferred_element_type=jnp.float32) * score_scale
    result = jnp.einsum(form[1], mixing(scores), value_part, preferred_element_type=jnp.float32)
    return result.astype(jnp.bfloat16), jnp.max(scores, axis=(0, 2, 3))


def plain_body(patch_tokens, projection):
    frames, positions, depth = patch_tokens.shape
    heads = projection.shape[-1] // HD
    parts = jnp.dot(
        patch_tokens.reshape(-1, depth), projection.reshape(depth, -1), preferred_element_type=jnp.float32
    )
    parts = parts.astype(jnp.bfloat16).reshape(frames, positions, 2, ROLES, heads, HD)
    space_out, space_high = plain_attention(
        ("fihd,fjhd->fhij", "fhij,fjhd->fihd"), *(parts[:, :, 0, r] for r in range(ROLES))
    )
    moved = [lax.all_to_all(parts[:, :, 1, r], "seq", split_axis=1, concat_axis=0, tiled=True) for r in range(ROLES)]
    time_out, time_high = plain_attention(("fphd,gphd->phfg", "phfg,gphd->fphd"), *moved)
    time_out = lax.all_to_all(time_out, "seq", split_axis=0, concat_axis=1, tiled=True)
    peak = lax.pmax(jnp.stack([space_high, time_high]), "seq")
    clip_factor = jnp.sqrt(clip_limit / jnp.maximum(peak, clip_limit))
    flat = (frames, positions, heads * HD)
    return space_out.reshape(flat), time_out.reshape(flat), clip_factor


def solution(mesh):
    seq, head = mesh.shape["seq"], mesh.shape["head"]

    def body(patch_tokens, projection):
        frames, positions, _ = patch_tokens.shape
        if seq == 8 and head == 4 and frames == 4 and positions % (16 * seq) == 0 and projection.shape[-1] <= 4 * HD:
            return fast_body(seq, head, patch_tokens, projection)
        return plain_body(patch_tokens, projection)

    return jax.shard_map(
        body,
        mesh=mesh,
        in_specs=(P("seq", None, None), P(None, None, None, "head")),
        out_specs=(P("seq", None, "head"), P("seq", None, "head"), P(None, "head")),
        check_vma=False,
    )
```

```python
import math

import jax
import jax.numpy as jnp
from jax import lax
from jax.experimental import pallas as pl
from jax.experimental.pallas import tpu as pltpu
from jax.sharding import PartitionSpec as P

HD = 128
ROLES = 3
clip_limit = 30.0
score_scale = 1.0 / math.sqrt(HD)
exp_scale = score_scale * math.log2(math.e)
VMEM = pl.BlockSpec(memory_space=pltpu.VMEM)
SMALL = pl.CostEstimate(flops=3000000000, bytes_accessed=8000000, transcendentals=0)
LARGE = pl.CostEstimate(flops=16000000000, bytes_accessed=40000000, transcendentals=0)
PARAMS = pltpu.CompilerParams(vmem_limit_bytes=32 * 1024 * 1024)


def in_hbm(value):
    return pltpu.with_memory_space_constraint(value, pltpu.HBM)


def dot_nt(a, b):
    return lax.dot_general(a, b, (((1,), (1,)), ((), ())), preferred_element_type=jnp.float32)


def attend(query_part, key_part, value_part, mask=None):
    raw = dot_nt(query_part, key_part)
    if mask is not None:
        raw = jnp.where(mask, raw, -jnp.inf)
    highest = jnp.max(raw, axis=-1, keepdims=True)
    expon = jnp.exp2((raw - highest) * exp_scale)
    weights = (expon * (1.0 / jnp.sum(expon, axis=-1, keepdims=True))).astype(jnp.bfloat16)
    result = jnp.dot(weights, value_part, preferred_element_type=jnp.float32)
    return result, jnp.max(highest, axis=0, keepdims=True)


def pick_matrix(which, chunk):
    rows = lax.broadcasted_iota(jnp.int32, (ROLES * chunk, ROLES * 2 * chunk), 0)
    cols = lax.broadcasted_iota(jnp.int32, (ROLES * chunk, ROLES * 2 * chunk), 1)
    source = ((rows % chunk) * ROLES + rows // chunk) * 2 + which
    return jnp.where(cols == source, 1.0, 0.0).astype(jnp.bfloat16)


def pick(pick_ref, w_ref, out_refs):
    depth, _, _, width = w_ref.shape
    chunk = pick_ref.shape[0] // ROLES
    span = 2 * ROLES * chunk
    flat = w_ref.reshape(depth * ROLES * 2, width)
    for i in range(depth // chunk):
        found = jnp.dot(pick_ref[...], flat[i * span : (i + 1) * span, :], preferred_element_type=jnp.float32)
        found = found.astype(jnp.bfloat16)
        for r in range(ROLES):
            out_refs[r][i * chunk : (i + 1) * chunk, :] = found[r * chunk : (r + 1) * chunk]


CHUNK = 64


def early_kernel(count, rows, index_ref, tokens_ref, w_ref, out_weights_ref, flag_ref, *refs):
    outs, (held, weights_ref, pick_ref, x_ref, w_sems, out_sems, x_sems) = refs[:count], refs[count:]
    frames, _, depth = tokens_ref.shape
    block = held.shape[1]
    steps = depth // block

    def load(step):
        return pltpu.make_async_copy(w_ref.at[pl.ds(step * block, block)], held.at[step % SLOTS], w_sems.at[step % SLOTS])

    def store(step):
        here = pl.ds(step * block, block)
        return pltpu.make_async_copy(weights_ref.at[here], out_weights_ref.at[here], out_sems.at[step])

    for step in range(SLOTS - 1):
        load(step).start()
    loads = []
    for i in range(count):
        start = pl.multiple_of(index_ref[i] * rows, rows)
        for f in range(frames):
            at = i * frames + f
            loads.append(
                pltpu.make_async_copy(
                    tokens_ref.at[f, pl.ds(start, rows)], x_ref.at[pl.ds(at * rows, rows)], x_sems.at[at]
                )
            )
            loads[-1].start()
    pick_ref[...] = pick_matrix(1, CHUNK)
    for step in range(steps):
        if step + SLOTS - 1 < steps:
            load(step + SLOTS - 1).start()
        load(step).wait()
        here = pl.ds(step * block, block)
        width = held.shape[-1]
        outs_at = [weights_ref.at[here, r * width : (r + 1) * width] for r in range(ROLES)]
        pick(pick_ref, held.at[step % SLOTS], outs_at)
        store(step).start()
    for copy in loads:
        copy.wait()
    total = jnp.dot(x_ref[...], weights_ref[...], preferred_element_type=jnp.float32)
    flag_ref[...] = jnp.zeros_like(flag_ref)
    for i, out in enumerate(outs):
        for pair in range(frames // 2):
            at = (i * frames + 2 * pair) * rows
            for g in range(rows // 8):
                out[g, pair * 16 : pair * 16 + 16, :] = pair_tiles(total, at, at + rows, g)
    for step in range(steps):
        store(step).wait()


def early(index, tokens, paired, rows, count):
    frames, _, depth = tokens.shape
    width = paired.shape[-1]
    cols = ROLES * width
    block = BLOCK
    out = jax.ShapeDtypeStruct((rows // 8, frames * 8, cols), jnp.bfloat16)
    here = count * frames * rows
    return pl.pallas_call(
        lambda *refs: early_kernel(count, rows, *refs),
        in_specs=[pl.BlockSpec(memory_space=pltpu.SMEM)] + [pl.BlockSpec(memory_space=pl.ANY)] * 2,
        out_specs=[pl.BlockSpec(memory_space=pl.ANY)] + [VMEM] * (1 + count),
        out_shape=[pltpu.HBM((depth, cols), jnp.bfloat16), jax.ShapeDtypeStruct((8, HD), jnp.float32)] + [out] * count,
        scratch_shapes=[
            pltpu.VMEM((SLOTS, block, ROLES, 2, width), jnp.bfloat16),
            pltpu.VMEM((depth, cols), jnp.bfloat16),
            pltpu.VMEM((ROLES * CHUNK, 2 * ROLES * CHUNK), jnp.bfloat16),
            pltpu.VMEM((here, depth), jnp.bfloat16),
            pltpu.SemaphoreType.DMA((SLOTS,)),
            pltpu.SemaphoreType.DMA((depth // block,)),
            pltpu.SemaphoreType.DMA((count * frames,)),
        ],
        compiler_params=PARAMS,
        cost_estimate=LARGE,
        name="early",
    )(index, in_hbm(tokens), in_hbm(paired))


BLOCK = 512
SLOTS = 3
SPLITS = 3


def space_peak_kernel(heads, x_hbm, w_hbm, flag_ref, parts_hbm, last_hbm, peak_ref, *scratch):
    held, x_ref, weights_ref, last_ref, parts_ref, pick_ref, w_sems, x_sem, last_sem, parts_sem = scratch
    frames, positions, depth = x_hbm.shape
    steps, block = held.shape[:2]
    width = heads * HD
    loads = [pltpu.make_async_copy(w_hbm.at[pl.ds(i * block, block)], held.at[i], w_sems.at[i]) for i in range(steps)]
    for load in loads:
        load.start()
    load_tokens = pltpu.make_async_copy(x_hbm, x_ref, x_sem.at[0])
    load_tokens.start()
    pick_ref[...] = pick_matrix(0, CHUNK)
    for step in range(steps):
        loads[step].wait()
        here = pl.ds(step * block, block)
        outs = [weights_ref.at[here, r * width : (r + 1) * width] for r in range(2)] + [last_ref.at[here]]
        pick(pick_ref, held.at[step], outs)
    store_last = pltpu.make_async_copy(last_ref, last_hbm, last_sem.at[0])
    store_last.start()
    load_tokens.wait()
    tokens = x_ref[...].reshape(frames * positions, depth)
    parts_ref[...] = jnp.dot(tokens, weights_ref[...], preferred_element_type=jnp.float32).astype(jnp.bfloat16)
    store = pltpu.make_async_copy(parts_ref, parts_hbm, parts_sem.at[0])
    store.start()
    for h in range(heads):
        peak = jnp.full((1, 1), -jnp.inf, jnp.float32)
        for f in range(frames):
            query_part, key_part = (
                parts_ref[f * positions : (f + 1) * positions, r * width + h * HD : r * width + (h + 1) * HD]
                for r in range(2)
            )
            peak = jnp.maximum(peak, jnp.max(dot_nt(query_part, key_part), keepdims=True))
        peak_ref[:, h * HD : (h + 1) * HD] = jnp.broadcast_to(peak * score_scale, (8, HD))
    store.wait()
    store_last.wait()


def space_peak(tokens, paired, flag, heads):
    frames, positions, depth = tokens.shape
    width = heads * HD
    rows = frames * positions
    block = BLOCK
    place = pl.BlockSpec(memory_space=pl.ANY)
    return pl.pallas_call(
        lambda *refs: space_peak_kernel(heads, *refs),
        in_specs=[place] * 3,
        out_specs=[place, place, VMEM],
        out_shape=[
            pltpu.HBM((rows, 2 * width), jnp.bfloat16),
            pltpu.HBM((depth, width), jnp.bfloat16),
            jax.ShapeDtypeStruct((8, width), jnp.float32),
        ],
        scratch_shapes=[
            pltpu.VMEM((depth // block, block, ROLES, 2, width), jnp.bfloat16),
            pltpu.VMEM(tokens.shape, jnp.bfloat16),
            pltpu.VMEM((depth, 2 * width), jnp.bfloat16),
            pltpu.VMEM((depth, width), jnp.bfloat16),
            pltpu.VMEM((rows, 2 * width), jnp.bfloat16),
            pltpu.VMEM((ROLES * CHUNK, 2 * ROLES * CHUNK), jnp.bfloat16),
            pltpu.SemaphoreType.DMA((depth // block,)),
            pltpu.SemaphoreType.DMA((1,)),
            pltpu.SemaphoreType.DMA((1,)),
            pltpu.SemaphoreType.DMA((1,)),
        ],
        compiler_params=pltpu.CompilerParams(vmem_limit_bytes=46 * 1024 * 1024),
        cost_estimate=SMALL,
        name="space_peak",
    )(in_hbm(tokens), in_hbm(paired), flag)


def space_kernel(heads, x_hbm, w_ref, parts_hbm, out_hbm, x_ref, parts_ref, out_ref, total, x_sems, parts_sem, out_sems):
    frames, positions, depth = x_hbm.shape
    width = heads * HD
    span = depth // SPLITS
    loads = []
    for split in range(SPLITS):
        here = pl.ds(split * span, span)
        loads.append([pltpu.make_async_copy(x_hbm.at[:, :, here], x_ref.at[:, :, here], x_sems.at[split])])
    loads.append([pltpu.make_async_copy(parts_hbm, parts_ref, parts_sem.at[0])])
    for group in loads:
        for copy in group:
            copy.start()
    for split in range(SPLITS):
        for copy in loads[split]:
            copy.wait()
        at = split * span
        tokens = x_ref[:, :, at : at + span].reshape(frames * positions, span)
        part = jnp.dot(tokens, w_ref[at : at + span, :], preferred_element_type=jnp.float32)
        total[...] = part if split == 0 else total[...] + part
    loads[-1][0].wait()
    stores = []
    for f in range(frames):
        rows = slice(f * positions, (f + 1) * positions)
        for h in range(heads):
            cols = [parts_ref[rows, r * width + h * HD : r * width + (h + 1) * HD] for r in range(2)]
            result, _ = attend(*cols, total[rows, h * HD : (h + 1) * HD].astype(jnp.bfloat16))
            out_ref[f, :, h * HD : (h + 1) * HD] = result.astype(jnp.bfloat16)
        stores.append(pltpu.make_async_copy(out_ref.at[f], out_hbm.at[f], out_sems.at[f]))
        stores[-1].start()
    for store in stores:
        store.wait()


def space_attention(tokens, weights, parts, heads):
    frames, positions, depth = tokens.shape
    width = heads * HD
    rows = frames * positions
    place = pl.BlockSpec(memory_space=pl.ANY)
    return pl.pallas_call(
        lambda *refs: space_kernel(heads, *refs),
        in_specs=[place, VMEM, place],
        out_specs=place,
        out_shape=jax.ShapeDtypeStruct((frames, positions, width), jnp.bfloat16),
        scratch_shapes=[
            pltpu.VMEM(tokens.shape, jnp.bfloat16),
            pltpu.VMEM((rows, 2 * width), jnp.bfloat16),
            pltpu.VMEM((frames, positions, width), jnp.bfloat16),
            pltpu.VMEM((rows, width), jnp.float32),
            pltpu.SemaphoreType.DMA((SPLITS,)),
            pltpu.SemaphoreType.DMA((1,)),
            pltpu.SemaphoreType.DMA((frames,)),
        ],
        compiler_params=PARAMS,
        cost_estimate=LARGE,
        name="space_attention",
    )(in_hbm(tokens), pltpu.with_memory_space_constraint(weights, pltpu.VMEM), in_hbm(parts))


def pieces(value):
    high = value.astype(jnp.bfloat16).astype(jnp.float32)
    mid = (value - high).astype(jnp.bfloat16).astype(jnp.float32)
    return high, mid, value - high - mid


def pair_tiles(total, one, two, group):
    tile = jnp.concatenate([total[at + group * 8 : at + group * 8 + 8] for at in (one, two)], axis=0)
    return tile.astype(jnp.bfloat16)


def project_kernel(blocks, rows, one_ref, two_ref, w_ref, out_ref):
    tokens = jnp.concatenate([one_ref[...], two_ref[...]], axis=0)
    total = jnp.dot(tokens, w_ref[...], preferred_element_type=jnp.float32)
    for g in range(rows // 8):
        for b in range(blocks):
            out_ref[g, b * 16 : b * 16 + 16, :] = pair_tiles(total, b * rows, (blocks + b) * rows, g)


def project(one, two, weights):
    blocks, rows, depth = one.shape
    return pl.pallas_call(
        lambda *refs: project_kernel(blocks, rows, *refs),
        in_specs=[VMEM] * 3,
        out_specs=VMEM,
        out_shape=jax.ShapeDtypeStruct((rows // 8, blocks * 16, weights.shape[1]), jnp.bfloat16),
        compiler_params=PARAMS,
        cost_estimate=LARGE,
        name="project",
    )(*[x.reshape(-1, depth) for x in (one, two)], pltpu.with_memory_space_constraint(weights, pltpu.VMEM))


def late_kernel(heads, spots, blocks_to, rows, *refs):
    (one_ref, two_ref, w_ref), ins, peak_ref = refs[:3], refs[3 : 3 + len(spots)], refs[3 + len(spots)]
    outs, parts_ref = refs[4 + len(spots) : -1], refs[-1]
    half = outs[0].shape[0]
    outs = [*outs[:2], outs[2].at[pl.ds(0, half)], outs[2].at[pl.ds(half, half)], *outs[3:]]
    blocks = len(blocks_to)
    tokens = jnp.concatenate([one_ref[...], two_ref[...]], axis=0)
    total = jnp.dot(tokens, w_ref[...], preferred_element_type=jnp.float32)
    for b in range(blocks):
        for g in range(rows // 8):
            parts_ref[g, b * 16 : b * 16 + 16, :] = pair_tiles(total, b * rows, (blocks + b) * rows, g)
    places = [place for spot in spots for place in spot] + [(d, 1) for d in blocks_to]
    attend_time(heads, places, [*ins, parts_ref], peak_ref, outs)


def attend_time(heads, spots, ins, peak_ref, outs):
    groups = ins[0].shape[0]
    width = heads * HD
    size = 16 * len(spots)
    row = lax.broadcasted_iota(jnp.int32, (size, size), 0)
    col = lax.broadcasted_iota(jnp.int32, (size, size), 1)
    mask = ((row ^ col) & 7) == 0
    line = lax.broadcasted_iota(jnp.int32, (16, HD), 0)
    lane = lax.broadcasted_iota(jnp.int32, (16, HD), 1) // TAIL
    tail = jnp.zeros((16, HD), jnp.float32)
    for h in range(heads):
        peak = jnp.full((1, 1), -jnp.inf, jnp.float32)
        results = []
        for g in range(groups):
            cols = []
            for r in range(ROLES):
                at = r * width + h * HD
                cols.append(jnp.concatenate([x[g, :, at : at + HD] for x in ins], axis=0))
            result, highest = attend(*cols, mask)
            peak = jnp.maximum(peak, highest * score_scale)
            results.append(result)
        for i, (out, pair) in enumerate(spots):
            for two in range(0, groups, 2):
                for k in range(2):
                    at = i * 16 + k * 8
                    tile = jnp.concatenate([results[two + j][at : at + 8] for j in range(2)], axis=0)
                    start = ((h * 4 + 2 * pair + k) * groups + two) * 8
                    outs[out][start : start + 16, :] = tile.astype(jnp.bfloat16)
        both = pieces(peak_ref[0:1, h * HD : (h + 1) * HD]) + pieces(jnp.broadcast_to(peak, (1, HD)))
        for i, value in enumerate(both):
            tail = jnp.where((line == i) & (lane == h), value, tail)
    for out in outs:
        out[heads * groups * 32 :, :] = tail.astype(jnp.bfloat16)


TAIL = 32


def late(one, two, weights, parts, spots, peaks, heads, count, blocks_to):
    blocks, rows, depth = one.shape
    cols = weights.shape[1]
    groups = rows // 8
    shape = (heads * groups * 32 + 16, HD)
    return pl.pallas_call(
        lambda *refs: late_kernel(heads, spots, blocks_to, rows, *refs),
        in_specs=[VMEM] * (4 + len(parts)),
        out_specs=[VMEM] * (count - 1),
        out_shape=[jax.ShapeDtypeStruct(shape, jnp.bfloat16)] * 2
        + [jax.ShapeDtypeStruct((2 * shape[0], HD), jnp.bfloat16)]
        + [jax.ShapeDtypeStruct(shape, jnp.bfloat16)] * (count - 4),
        scratch_shapes=[
            pltpu.VMEM((groups, blocks * 16, cols), jnp.bfloat16),
        ],
        compiler_params=PARAMS,
        cost_estimate=LARGE,
        name="late",
    )(
        *[x.reshape(-1, depth) for x in (one, two)],
        pltpu.with_memory_space_constraint(weights, pltpu.VMEM),
        *parts,
        peaks,
    )


def finish_kernel(direct, heads, index_ref, *refs):
    ins, out_ref, clip_ref = refs[:-2], refs[-2], refs[-1]
    half = ins[0].shape[0]
    near = [ins[0], ins[1].at[pl.ds(0, half)], ins[2].at[pl.ds(0, half)], ins[2].at[pl.ds(half, half)]]
    ins = [*near, *ins[3:]]
    rows = (half - 16) // (4 * heads)
    mine = index_ref[0]
    peak = None
    for d, source in enumerate(ins):
        start = pl.multiple_of(index_ref[1 + d] * rows, rows)
        for h in range(heads):
            for pair in range(2):
                for k in range(2):
                    frame = 2 * pair + k if d in direct else mine ^ (pair + 2 * k)
                    at = (h * 4 + 2 * pair + k) * rows
                    out_ref[frame, pl.ds(start, rows), h * HD : (h + 1) * HD] = source[at : at + rows, :]
        tail = source[half - 16 :, :].astype(jnp.float32)
        values = [tail[3 * a : 3 * a + 1] + tail[3 * a + 1 : 3 * a + 2] + tail[3 * a + 2 : 3 * a + 3] for a in range(2)]
        peak = values if peak is None else [jnp.maximum(p, v) for p, v in zip(peak, values)]
    for a in range(2):
        clip = jnp.sqrt(clip_limit / jnp.maximum(peak[a], clip_limit))
        clip_ref[a : a + 1, :] = jnp.concatenate([clip[:, h * TAIL : h * TAIL + 1] for h in range(heads)], axis=1)


def finish(index, received, frames, positions, direct, heads):
    return pl.pallas_call(
        lambda *refs: finish_kernel(direct, heads, *refs),
        in_specs=[pl.BlockSpec(memory_space=pltpu.SMEM)] + [VMEM] * len(received),
        out_specs=[VMEM, VMEM],
        out_shape=[
            jax.ShapeDtypeStruct((frames, positions, heads * HD), jnp.bfloat16),
            jax.ShapeDtypeStruct((2, heads), jnp.float32),
        ],
        compiler_params=PARAMS,
        name="finish",
    )(index, *received)


def swap(value, axis, size, distance):
    return lax.ppermute(value, axis, [(i, i ^ distance) for i in range(size)])


def fast_body(seq, head, patch_tokens, projection):
    frames, positions, depth = patch_tokens.shape
    heads = projection.shape[-1] // HD
    width = heads * HD
    rows = positions // seq
    me, mine = lax.axis_index("seq"), lax.axis_index("head")
    token_group, direct = (3, 2, 5, 4), (6, 7, 1)
    paired = jnp.transpose(projection, (0, 2, 1, 3))

    def piece(frame, owner):
        return lax.dynamic_slice(patch_tokens, (frame, owner * rows, 0), (1, rows, depth))

    got = [swap(piece(mine, me ^ d), "seq", seq, d) for d in token_group]
    index = jnp.stack([me ^ d for d in (*direct, 0)]).astype(jnp.int32)
    weights, flag, *away, own = early(index, patch_tokens, paired, rows, len(direct) + 1)
    away = [swap(part, "seq", seq, d) for d, part in zip(direct, away)]

    *got, flag = lax.optimization_barrier([*got, flag])
    here = jnp.concatenate(got, axis=0)
    there = swap(here, "head", head, 2)
    parts, last, peaks = space_peak(patch_tokens, paired, flag, heads)
    here, there, peaks = lax.optimization_barrier([here, there, peaks])
    here_other = swap(here, "head", head, 1)
    there_other = swap(there, "head", head, 1)
    first = project(here, there, weights)
    spots = [[(d, 0), (d, 1)] for d in (*direct, 0)] + [[(d, 0) for d in token_group]]
    outs = late(here_other, there_other, weights, [*away, own, first], spots, peaks, heads, seq, token_group)
    *outs, parts = lax.optimization_barrier([*outs, parts])
    mine_out, x_out, z_out, *far_outs = outs
    half = mine_out.shape[0]
    z_pair = swap(z_out, "seq", seq, 2)
    far_pairs = [swap(out, "seq", seq, d) for d, out in zip((4, 5, 6, 7), far_outs)]
    x_pair = swap(jnp.concatenate([x_out, z_pair[half:]], axis=0), "seq", seq, 1)
    received = [mine_out, z_pair, x_pair, *far_pairs]
    order = (0, 2, 1, 3, 4, 5, 6, 7)
    space_out = space_attention(patch_tokens, last, parts, heads)
    finish_index = jnp.stack([mine] + [me ^ d for d in order]).astype(jnp.int32)
    natural = [i for i, d in enumerate(order) if d not in token_group]
    time_out, clip = finish(finish_index, received, frames, positions, natural, heads)
    return space_out, time_out, clip


def mixing(scores):
    highest = jnp.max(scores, axis=-1, keepdims=True)
    expon = jnp.exp(scores - highest)
    return (expon / jnp.sum(expon, axis=-1, keepdims=True)).astype(jnp.bfloat16)


def plain_attention(form, query_part, key_part, value_part):
    scores = jnp.einsum(form[0], query_part, key_part, preferred_element_type=jnp.float32) * score_scale
    result = jnp.einsum(form[1], mixing(scores), value_part, preferred_element_type=jnp.float32)
    return result.astype(jnp.bfloat16), jnp.max(scores, axis=(0, 2, 3))


def plain_body(patch_tokens, projection):
    frames, positions, depth = patch_tokens.shape
    heads = projection.shape[-1] // HD
    parts = jnp.dot(
        patch_tokens.reshape(-1, depth), projection.reshape(depth, -1), preferred_element_type=jnp.float32
    )
    parts = parts.astype(jnp.bfloat16).reshape(frames, positions, 2, ROLES, heads, HD)
    space_out, space_high = plain_attention(
        ("fihd,fjhd->fhij", "fhij,fjhd->fihd"), *(parts[:, :, 0, r] for r in range(ROLES))
    )
    moved = [lax.all_to_all(parts[:, :, 1, r], "seq", split_axis=1, concat_axis=0, tiled=True) for r in range(ROLES)]
    time_out, time_high = plain_attention(("fphd,gphd->phfg", "phfg,gphd->fphd"), *moved)
    time_out = lax.all_to_all(time_out, "seq", split_axis=0, concat_axis=1, tiled=True)
    peak = lax.pmax(jnp.stack([space_high, time_high]), "seq")
    clip_factor = jnp.sqrt(clip_limit / jnp.maximum(peak, clip_limit))
    flat = (frames, positions, heads * HD)
    return space_out.reshape(flat), time_out.reshape(flat), clip_factor


def solution(mesh):
    seq, head = mesh.shape["seq"], mesh.shape["head"]

    def body(patch_tokens, projection):
        frames, positions, _ = patch_tokens.shape
        if seq == 8 and head == 4 and frames == 4 and positions % (16 * seq) == 0 and projection.shape[-1] <= 4 * HD:
            return fast_body(seq, head, patch_tokens, projection)
        return plain_body(patch_tokens, projection)

    return jax.shard_map(
        body,
        mesh=mesh,
        in_specs=(P("seq", None, None), P(None, None, None, "head")),
        out_specs=(P("seq", None, "head"), P("seq", None, "head"), P(None, "head")),
        check_vma=False,
    )
```

```python
import math

import jax
import jax.numpy as jnp
from jax import lax
from jax.experimental import pallas as pl
from jax.experimental.pallas import tpu as pltpu
from jax.sharding import PartitionSpec as P

HD = 128
ROLES = 3
clip_limit = 30.0
score_scale = 1.0 / math.sqrt(HD)
exp_scale = score_scale * math.log2(math.e)
VMEM = pl.BlockSpec(memory_space=pltpu.VMEM)
SMALL = pl.CostEstimate(flops=3000000000, bytes_accessed=8000000, transcendentals=0)
LARGE = pl.CostEstimate(flops=16000000000, bytes_accessed=40000000, transcendentals=0)
PARAMS = pltpu.CompilerParams(vmem_limit_bytes=32 * 1024 * 1024)


def in_hbm(value):
    return pltpu.with_memory_space_constraint(value, pltpu.HBM)


def dot_nt(a, b):
    return lax.dot_general(a, b, (((1,), (1,)), ((), ())), preferred_element_type=jnp.float32)


def attend(query_part, key_part, value_part, mask=None):
    raw = dot_nt(query_part, key_part)
    if mask is not None:
        raw = jnp.where(mask, raw, -jnp.inf)
    highest = jnp.max(raw, axis=-1, keepdims=True)
    expon = jnp.exp2((raw - highest) * exp_scale)
    weights = (expon * (1.0 / jnp.sum(expon, axis=-1, keepdims=True))).astype(jnp.bfloat16)
    result = jnp.dot(weights, value_part, preferred_element_type=jnp.float32)
    return result, jnp.max(highest, axis=0, keepdims=True)


def pick_matrix(which, chunk):
    rows = lax.broadcasted_iota(jnp.int32, (ROLES * chunk, ROLES * 2 * chunk), 0)
    cols = lax.broadcasted_iota(jnp.int32, (ROLES * chunk, ROLES * 2 * chunk), 1)
    source = ((rows % chunk) * ROLES + rows // chunk) * 2 + which
    return jnp.where(cols == source, 1.0, 0.0).astype(jnp.bfloat16)


def pick(pick_ref, w_ref, out_refs):
    depth, _, _, width = w_ref.shape
    chunk = pick_ref.shape[0] // ROLES
    span = 2 * ROLES * chunk
    flat = w_ref.reshape(depth * ROLES * 2, width)
    for i in range(depth // chunk):
        found = jnp.dot(pick_ref[...], flat[i * span : (i + 1) * span, :], preferred_element_type=jnp.float32)
        found = found.astype(jnp.bfloat16)
        for r in range(ROLES):
            out_refs[r][i * chunk : (i + 1) * chunk, :] = found[r * chunk : (r + 1) * chunk]


CHUNK = 64


def early_kernel(count, rows, index_ref, tokens_ref, w_ref, out_weights_ref, flag_ref, *refs):
    outs, (held, weights_ref, pick_ref, x_ref, w_sems, out_sems, x_sems) = refs[:count], refs[count:]
    frames, _, depth = tokens_ref.shape
    block = held.shape[1]
    steps = depth // block

    def load(step):
        return pltpu.make_async_copy(w_ref.at[pl.ds(step * block, block)], held.at[step % SLOTS], w_sems.at[step % SLOTS])

    def store(step):
        here = pl.ds(step * block, block)
        return pltpu.make_async_copy(weights_ref.at[here], out_weights_ref.at[here], out_sems.at[step])

    for step in range(SLOTS - 1):
        load(step).start()
    loads = []
    for i in range(count):
        start = pl.multiple_of(index_ref[i] * rows, rows)
        for f in range(frames):
            at = i * frames + f
            loads.append(
                pltpu.make_async_copy(
                    tokens_ref.at[f, pl.ds(start, rows)], x_ref.at[pl.ds(at * rows, rows)], x_sems.at[at]
                )
            )
            loads[-1].start()
    pick_ref[...] = pick_matrix(1, CHUNK)
    for step in range(steps):
        if step + SLOTS - 1 < steps:
            load(step + SLOTS - 1).start()
        load(step).wait()
        here = pl.ds(step * block, block)
        width = held.shape[-1]
        outs_at = [weights_ref.at[here, r * width : (r + 1) * width] for r in range(ROLES)]
        pick(pick_ref, held.at[step % SLOTS], outs_at)
        store(step).start()
    for copy in loads:
        copy.wait()
    total = jnp.dot(x_ref[...], weights_ref[...], preferred_element_type=jnp.float32)
    flag_ref[...] = jnp.zeros_like(flag_ref)
    for i, out in enumerate(outs):
        for pair in range(frames // 2):
            at = (i * frames + 2 * pair) * rows
            for g in range(rows // 8):
                out[g, pair * 16 : pair * 16 + 16, :] = pair_tiles(total, at, at + rows, g)
    for step in range(steps):
        store(step).wait()


def early(index, tokens, paired, rows, count):
    frames, _, depth = tokens.shape
    width = paired.shape[-1]
    cols = ROLES * width
    block = BLOCK
    out = jax.ShapeDtypeStruct((rows // 8, frames * 8, cols), jnp.bfloat16)
    here = count * frames * rows
    return pl.pallas_call(
        lambda *refs: early_kernel(count, rows, *refs),
        in_specs=[pl.BlockSpec(memory_space=pltpu.SMEM)] + [pl.BlockSpec(memory_space=pl.ANY)] * 2,
        out_specs=[pl.BlockSpec(memory_space=pl.ANY)] + [VMEM] * (1 + count),
        out_shape=[pltpu.HBM((depth, cols), jnp.bfloat16), jax.ShapeDtypeStruct((8, HD), jnp.float32)] + [out] * count,
        scratch_shapes=[
            pltpu.VMEM((SLOTS, block, ROLES, 2, width), jnp.bfloat16),
            pltpu.VMEM((depth, cols), jnp.bfloat16),
            pltpu.VMEM((ROLES * CHUNK, 2 * ROLES * CHUNK), jnp.bfloat16),
            pltpu.VMEM((here, depth), jnp.bfloat16),
            pltpu.SemaphoreType.DMA((SLOTS,)),
            pltpu.SemaphoreType.DMA((depth // block,)),
            pltpu.SemaphoreType.DMA((count * frames,)),
        ],
        compiler_params=PARAMS,
        cost_estimate=LARGE,
        name="early",
    )(index, in_hbm(tokens), in_hbm(paired))


BLOCK = 512
SLOTS = 3
SPLITS = 3


def space_peak_kernel(heads, x_hbm, w_hbm, flag_ref, parts_hbm, last_hbm, peak_ref, *scratch):
    held, x_ref, weights_ref, last_ref, parts_ref, pick_ref, w_sems, x_sem, last_sem, parts_sem = scratch
    frames, positions, depth = x_hbm.shape
    steps, block = held.shape[:2]
    width = heads * HD
    loads = [pltpu.make_async_copy(w_hbm.at[pl.ds(i * block, block)], held.at[i], w_sems.at[i]) for i in range(steps)]
    for load in loads:
        load.start()
    load_tokens = pltpu.make_async_copy(x_hbm, x_ref, x_sem.at[0])
    load_tokens.start()
    pick_ref[...] = pick_matrix(0, CHUNK)
    for step in range(steps):
        loads[step].wait()
        here = pl.ds(step * block, block)
        outs = [weights_ref.at[here, r * width : (r + 1) * width] for r in range(2)] + [last_ref.at[here]]
        pick(pick_ref, held.at[step], outs)
    store_last = pltpu.make_async_copy(last_ref, last_hbm, last_sem.at[0])
    store_last.start()
    load_tokens.wait()
    tokens = x_ref[...].reshape(frames * positions, depth)
    parts_ref[...] = jnp.dot(tokens, weights_ref[...], preferred_element_type=jnp.float32).astype(jnp.bfloat16)
    store = pltpu.make_async_copy(parts_ref, parts_hbm, parts_sem.at[0])
    store.start()
    for h in range(heads):
        peak = jnp.full((1, 1), -jnp.inf, jnp.float32)
        for f in range(frames):
            query_part, key_part = (
                parts_ref[f * positions : (f + 1) * positions, r * width + h * HD : r * width + (h + 1) * HD]
                for r in range(2)
            )
            peak = jnp.maximum(peak, jnp.max(dot_nt(query_part, key_part), keepdims=True))
        peak_ref[:, h * HD : (h + 1) * HD] = jnp.broadcast_to(peak * score_scale, (8, HD))
    store.wait()
    store_last.wait()


def space_peak(tokens, paired, flag, heads):
    frames, positions, depth = tokens.shape
    width = heads * HD
    rows = frames * positions
    block = BLOCK
    place = pl.BlockSpec(memory_space=pl.ANY)
    return pl.pallas_call(
        lambda *refs: space_peak_kernel(heads, *refs),
        in_specs=[place] * 3,
        out_specs=[place, place, VMEM],
        out_shape=[
            pltpu.HBM((rows, 2 * width), jnp.bfloat16),
            pltpu.HBM((depth, width), jnp.bfloat16),
            jax.ShapeDtypeStruct((8, width), jnp.float32),
        ],
        scratch_shapes=[
            pltpu.VMEM((depth // block, block, ROLES, 2, width), jnp.bfloat16),
            pltpu.VMEM(tokens.shape, jnp.bfloat16),
            pltpu.VMEM((depth, 2 * width), jnp.bfloat16),
            pltpu.VMEM((depth, width), jnp.bfloat16),
            pltpu.VMEM((rows, 2 * width), jnp.bfloat16),
            pltpu.VMEM((ROLES * CHUNK, 2 * ROLES * CHUNK), jnp.bfloat16),
            pltpu.SemaphoreType.DMA((depth // block,)),
            pltpu.SemaphoreType.DMA((1,)),
            pltpu.SemaphoreType.DMA((1,)),
            pltpu.SemaphoreType.DMA((1,)),
        ],
        compiler_params=pltpu.CompilerParams(vmem_limit_bytes=46 * 1024 * 1024),
        cost_estimate=SMALL,
        name="space_peak",
    )(in_hbm(tokens), in_hbm(paired), flag)


def space_kernel(heads, x_hbm, w_ref, parts_hbm, out_hbm, x_ref, parts_ref, out_ref, total, x_sems, parts_sem, out_sems):
    frames, positions, depth = x_hbm.shape
    width = heads * HD
    span = depth // SPLITS
    loads = []
    for split in range(SPLITS):
        here = pl.ds(split * span, span)
        loads.append([pltpu.make_async_copy(x_hbm.at[:, :, here], x_ref.at[:, :, here], x_sems.at[split])])
    loads.append([pltpu.make_async_copy(parts_hbm, parts_ref, parts_sem.at[0])])
    for group in loads:
        for copy in group:
            copy.start()
    for split in range(SPLITS):
        for copy in loads[split]:
            copy.wait()
        at = split * span
        tokens = x_ref[:, :, at : at + span].reshape(frames * positions, span)
        part = jnp.dot(tokens, w_ref[at : at + span, :], preferred_element_type=jnp.float32)
        total[...] = part if split == 0 else total[...] + part
    loads[-1][0].wait()
    stores = []
    for f in range(frames):
        rows = slice(f * positions, (f + 1) * positions)
        for h in range(heads):
            cols = [parts_ref[rows, r * width + h * HD : r * width + (h + 1) * HD] for r in range(2)]
            result, _ = attend(*cols, total[rows, h * HD : (h + 1) * HD].astype(jnp.bfloat16))
            out_ref[f, :, h * HD : (h + 1) * HD] = result.astype(jnp.bfloat16)
        stores.append(pltpu.make_async_copy(out_ref.at[f], out_hbm.at[f], out_sems.at[f]))
        stores[-1].start()
    for store in stores:
        store.wait()


def space_attention(tokens, weights, parts, heads):
    frames, positions, depth = tokens.shape
    width = heads * HD
    rows = frames * positions
    place = pl.BlockSpec(memory_space=pl.ANY)
    return pl.pallas_call(
        lambda *refs: space_kernel(heads, *refs),
        in_specs=[place, VMEM, place],
        out_specs=place,
        out_shape=jax.ShapeDtypeStruct((frames, positions, width), jnp.bfloat16),
        scratch_shapes=[
            pltpu.VMEM(tokens.shape, jnp.bfloat16),
            pltpu.VMEM((rows, 2 * width), jnp.bfloat16),
            pltpu.VMEM((frames, positions, width), jnp.bfloat16),
            pltpu.VMEM((rows, width), jnp.float32),
            pltpu.SemaphoreType.DMA((SPLITS,)),
            pltpu.SemaphoreType.DMA((1,)),
            pltpu.SemaphoreType.DMA((frames,)),
        ],
        compiler_params=PARAMS,
        cost_estimate=LARGE,
        name="space_attention",
    )(in_hbm(tokens), pltpu.with_memory_space_constraint(weights, pltpu.VMEM), in_hbm(parts))


def pieces(value):
    high = value.astype(jnp.bfloat16).astype(jnp.float32)
    mid = (value - high).astype(jnp.bfloat16).astype(jnp.float32)
    return high, mid, value - high - mid


def pair_tiles(total, one, two, group):
    tile = jnp.concatenate([total[at + group * 8 : at + group * 8 + 8] for at in (one, two)], axis=0)
    return tile.astype(jnp.bfloat16)


def project_kernel(blocks, rows, one_ref, two_ref, w_ref, out_ref):
    tokens = jnp.concatenate([one_ref[...], two_ref[...]], axis=0)
    total = jnp.dot(tokens, w_ref[...], preferred_element_type=jnp.float32)
    for g in range(rows // 8):
        for b in range(blocks):
            out_ref[g, b * 16 : b * 16 + 16, :] = pair_tiles(total, b * rows, (blocks + b) * rows, g)


def project(one, two, weights):
    blocks, rows, depth = one.shape
    return pl.pallas_call(
        lambda *refs: project_kernel(blocks, rows, *refs),
        in_specs=[VMEM] * 3,
        out_specs=VMEM,
        out_shape=jax.ShapeDtypeStruct((rows // 8, blocks * 16, weights.shape[1]), jnp.bfloat16),
        compiler_params=PARAMS,
        cost_estimate=LARGE,
        name="project",
    )(*[x.reshape(-1, depth) for x in (one, two)], pltpu.with_memory_space_constraint(weights, pltpu.VMEM))


def late_kernel(heads, spots, blocks_to, rows, *refs):
    (one_ref, two_ref, w_ref), ins, peak_ref = refs[:3], refs[3 : 3 + len(spots)], refs[3 + len(spots)]
    outs, parts_ref = refs[4 + len(spots) : -1], refs[-1]
    half = outs[0].shape[0]
    outs = [*outs[:2], outs[2].at[pl.ds(0, half)], outs[2].at[pl.ds(half, half)], *outs[3:]]
    blocks = len(blocks_to)
    tokens = jnp.concatenate([one_ref[...], two_ref[...]], axis=0)
    total = jnp.dot(tokens, w_ref[...], preferred_element_type=jnp.float32)
    for b in range(blocks):
        for g in range(rows // 8):
            parts_ref[g, b * 16 : b * 16 + 16, :] = pair_tiles(total, b * rows, (blocks + b) * rows, g)
    places = [place for spot in spots for place in spot] + [(d, 1) for d in blocks_to]
    attend_time(heads, places, [*ins, parts_ref], peak_ref, outs)


def attend_time(heads, spots, ins, peak_ref, outs):
    groups = ins[0].shape[0]
    width = heads * HD
    size = 16 * len(spots)
    row = lax.broadcasted_iota(jnp.int32, (size, size), 0)
    col = lax.broadcasted_iota(jnp.int32, (size, size), 1)
    mask = ((row ^ col) & 7) == 0
    line = lax.broadcasted_iota(jnp.int32, (16, HD), 0)
    lane = lax.broadcasted_iota(jnp.int32, (16, HD), 1) // TAIL
    tail = jnp.zeros((16, HD), jnp.float32)
    for h in range(heads):
        peak = jnp.full((1, 1), -jnp.inf, jnp.float32)
        results = []
        for g in range(groups):
            cols = []
            for r in range(ROLES):
                at = r * width + h * HD
                cols.append(jnp.concatenate([x[g, :, at : at + HD] for x in ins], axis=0))
            result, highest = attend(*cols, mask)
            peak = jnp.maximum(peak, highest * score_scale)
            results.append(result)
        for i, (out, pair) in enumerate(spots):
            for two in range(0, groups, 2):
                for k in range(2):
                    at = i * 16 + k * 8
                    tile = jnp.concatenate([results[two + j][at : at + 8] for j in range(2)], axis=0)
                    start = ((h * 4 + 2 * pair + k) * groups + two) * 8
                    outs[out][start : start + 16, :] = tile.astype(jnp.bfloat16)
        both = pieces(peak_ref[0:1, h * HD : (h + 1) * HD]) + pieces(jnp.broadcast_to(peak, (1, HD)))
        for i, value in enumerate(both):
            tail = jnp.where((line == i) & (lane == h), value, tail)
    for out in outs:
        out[heads * groups * 32 :, :] = tail.astype(jnp.bfloat16)


TAIL = 32


def late(one, two, weights, parts, spots, peaks, heads, count, blocks_to):
    blocks, rows, depth = one.shape
    cols = weights.shape[1]
    groups = rows // 8
    shape = (heads * groups * 32 + 16, HD)
    return pl.pallas_call(
        lambda *refs: late_kernel(heads, spots, blocks_to, rows, *refs),
        in_specs=[VMEM] * (4 + len(parts)),
        out_specs=[VMEM] * (count - 1),
        out_shape=[jax.ShapeDtypeStruct(shape, jnp.bfloat16)] * 2
        + [jax.ShapeDtypeStruct((2 * shape[0], HD), jnp.bfloat16)]
        + [jax.ShapeDtypeStruct(shape, jnp.bfloat16)] * (count - 4),
        scratch_shapes=[
            pltpu.VMEM((groups, blocks * 16, cols), jnp.bfloat16),
        ],
        compiler_params=PARAMS,
        cost_estimate=LARGE,
        name="late",
    )(
        *[x.reshape(-1, depth) for x in (one, two)],
        pltpu.with_memory_space_constraint(weights, pltpu.VMEM),
        *parts,
        peaks,
    )


def finish_kernel(direct, heads, index_ref, *refs):
    ins, out_ref, clip_ref = refs[:-2], refs[-2], refs[-1]
    half = ins[0].shape[0]
    near = [ins[0], ins[1].at[pl.ds(0, half)], ins[2].at[pl.ds(0, half)], ins[2].at[pl.ds(half, half)]]
    ins = [*near, *ins[3:]]
    rows = (half - 16) // (4 * heads)
    mine = index_ref[0]
    peak = None
    for d, source in enumerate(ins):
        start = pl.multiple_of(index_ref[1 + d] * rows, rows)
        for h in range(heads):
            for pair in range(2):
                for k in range(2):
                    frame = 2 * pair + k if d in direct else mine ^ (pair + 2 * k)
                    at = (h * 4 + 2 * pair + k) * rows
                    out_ref[frame, pl.ds(start, rows), h * HD : (h + 1) * HD] = source[at : at + rows, :]
        tail = source[half - 16 :, :].astype(jnp.float32)
        values = [tail[3 * a : 3 * a + 1] + tail[3 * a + 1 : 3 * a + 2] + tail[3 * a + 2 : 3 * a + 3] for a in range(2)]
        peak = values if peak is None else [jnp.maximum(p, v) for p, v in zip(peak, values)]
    for a in range(2):
        clip = jnp.sqrt(clip_limit / jnp.maximum(peak[a], clip_limit))
        clip_ref[a : a + 1, :] = jnp.concatenate([clip[:, h * TAIL : h * TAIL + 1] for h in range(heads)], axis=1)


def finish(index, received, frames, positions, direct, heads):
    return pl.pallas_call(
        lambda *refs: finish_kernel(direct, heads, *refs),
        in_specs=[pl.BlockSpec(memory_space=pltpu.SMEM)] + [VMEM] * len(received),
        out_specs=[VMEM, VMEM],
        out_shape=[
            jax.ShapeDtypeStruct((frames, positions, heads * HD), jnp.bfloat16),
            jax.ShapeDtypeStruct((2, heads), jnp.float32),
        ],
        compiler_params=PARAMS,
        name="finish",
    )(index, *received)


def swap(value, axis, size, distance):
    return lax.ppermute(value, axis, [(i, i ^ distance) for i in range(size)])


def fast_body(seq, head, patch_tokens, projection):
    frames, positions, depth = patch_tokens.shape
    heads = projection.shape[-1] // HD
    width = heads * HD
    rows = positions // seq
    me, mine = lax.axis_index("seq"), lax.axis_index("head")
    token_group, direct = (3, 2, 5, 4), (1, 6, 7)
    paired = jnp.transpose(projection, (0, 2, 1, 3))

    def piece(frame, owner):
        return lax.dynamic_slice(patch_tokens, (frame, owner * rows, 0), (1, rows, depth))

    got = [swap(piece(mine, me ^ d), "seq", seq, d) for d in token_group]
    index = jnp.stack([me ^ d for d in (*direct, 0)]).astype(jnp.int32)
    weights, flag, *away, own = early(index, patch_tokens, paired, rows, len(direct) + 1)
    away = [swap(part, "seq", seq, d) for d, part in zip(direct, away)]

    *got, flag = lax.optimization_barrier([*got, flag])
    here = jnp.concatenate(got, axis=0)
    there = swap(here, "head", head, 2)
    parts, last, peaks = space_peak(patch_tokens, paired, flag, heads)
    here, there, peaks = lax.optimization_barrier([here, there, peaks])
    here_other = swap(here, "head", head, 1)
    there_other = swap(there, "head", head, 1)
    first = project(here, there, weights)
    spots = [[(d, 0), (d, 1)] for d in (*direct, 0)] + [[(d, 0) for d in token_group]]
    outs = late(here_other, there_other, weights, [*away, own, first], spots, peaks, heads, seq, token_group)
    *outs, parts = lax.optimization_barrier([*outs, parts])
    mine_out, x_out, z_out, *far_outs = outs
    half = mine_out.shape[0]
    z_pair = swap(z_out, "seq", seq, 2)
    far_pairs = [swap(out, "seq", seq, d) for d, out in zip((4, 5, 6, 7), far_outs)]
    x_pair = swap(jnp.concatenate([x_out, z_pair[half:]], axis=0), "seq", seq, 1)
    received = [mine_out, z_pair, x_pair, *far_pairs]
    order = (0, 2, 1, 3, 4, 5, 6, 7)
    space_out = space_attention(patch_tokens, last, parts, heads)
    finish_index = jnp.stack([mine] + [me ^ d for d in order]).astype(jnp.int32)
    natural = [i for i, d in enumerate(order) if d not in token_group]
    time_out, clip = finish(finish_index, received, frames, positions, natural, heads)
    return space_out, time_out, clip


def mixing(scores):
    highest = jnp.max(scores, axis=-1, keepdims=True)
    expon = jnp.exp(scores - highest)
    return (expon / jnp.sum(expon, axis=-1, keepdims=True)).astype(jnp.bfloat16)


def plain_attention(form, query_part, key_part, value_part):
    scores = jnp.einsum(form[0], query_part, key_part, preferred_element_type=jnp.float32) * score_scale
    result = jnp.einsum(form[1], mixing(scores), value_part, preferred_element_type=jnp.float32)
    return result.astype(jnp.bfloat16), jnp.max(scores, axis=(0, 2, 3))


def plain_body(patch_tokens, projection):
    frames, positions, depth = patch_tokens.shape
    heads = projection.shape[-1] // HD
    parts = jnp.dot(
        patch_tokens.reshape(-1, depth), projection.reshape(depth, -1), preferred_element_type=jnp.float32
    )
    parts = parts.astype(jnp.bfloat16).reshape(frames, positions, 2, ROLES, heads, HD)
    space_out, space_high = plain_attention(
        ("fihd,fjhd->fhij", "fhij,fjhd->fihd"), *(parts[:, :, 0, r] for r in range(ROLES))
    )
    moved = [lax.all_to_all(parts[:, :, 1, r], "seq", split_axis=1, concat_axis=0, tiled=True) for r in range(ROLES)]
    time_out, time_high = plain_attention(("fphd,gphd->phfg", "phfg,gphd->fphd"), *moved)
    time_out = lax.all_to_all(time_out, "seq", split_axis=0, concat_axis=1, tiled=True)
    peak = lax.pmax(jnp.stack([space_high, time_high]), "seq")
    clip_factor = jnp.sqrt(clip_limit / jnp.maximum(peak, clip_limit))
    flat = (frames, positions, heads * HD)
    return space_out.reshape(flat), time_out.reshape(flat), clip_factor


def solution(mesh):
    seq, head = mesh.shape["seq"], mesh.shape["head"]

    def body(patch_tokens, projection):
        frames, positions, _ = patch_tokens.shape
        if seq == 8 and head == 4 and frames == 4 and positions % (16 * seq) == 0 and projection.shape[-1] <= 4 * HD:
            return fast_body(seq, head, patch_tokens, projection)
        return plain_body(patch_tokens, projection)

    return jax.shard_map(
        body,
        mesh=mesh,
        in_specs=(P("seq", None, None), P(None, None, None, "head")),
        out_specs=(P("seq", None, "head"), P("seq", None, "head"), P(None, "head")),
        check_vma=False,
    )
```

```python
import math

import jax
import jax.numpy as jnp
from jax import lax
from jax.experimental import pallas as pl
from jax.experimental.pallas import tpu as pltpu
from jax.sharding import PartitionSpec as P

HD = 128
ROLES = 3
clip_limit = 30.0
score_scale = 1.0 / math.sqrt(HD)
exp_scale = score_scale * math.log2(math.e)
VMEM = pl.BlockSpec(memory_space=pltpu.VMEM)
SMALL = pl.CostEstimate(flops=3000000000, bytes_accessed=8000000, transcendentals=0)
LARGE = pl.CostEstimate(flops=16000000000, bytes_accessed=40000000, transcendentals=0)
PARAMS = pltpu.CompilerParams(vmem_limit_bytes=32 * 1024 * 1024)


def in_hbm(value):
    return pltpu.with_memory_space_constraint(value, pltpu.HBM)


def dot_nt(a, b):
    return lax.dot_general(a, b, (((1,), (1,)), ((), ())), preferred_element_type=jnp.float32)


def attend(query_part, key_part, value_part, mask=None):
    raw = dot_nt(query_part, key_part)
    if mask is not None:
        raw = jnp.where(mask, raw, -jnp.inf)
    highest = jnp.max(raw, axis=-1, keepdims=True)
    expon = jnp.exp2((raw - highest) * exp_scale)
    weights = (expon * (1.0 / jnp.sum(expon, axis=-1, keepdims=True))).astype(jnp.bfloat16)
    result = jnp.dot(weights, value_part, preferred_element_type=jnp.float32)
    return result, jnp.max(highest, axis=0, keepdims=True)


def pick_matrix(which, chunk):
    rows = lax.broadcasted_iota(jnp.int32, (ROLES * chunk, ROLES * 2 * chunk), 0)
    cols = lax.broadcasted_iota(jnp.int32, (ROLES * chunk, ROLES * 2 * chunk), 1)
    source = ((rows % chunk) * ROLES + rows // chunk) * 2 + which
    return jnp.where(cols == source, 1.0, 0.0).astype(jnp.bfloat16)


def pick(pick_ref, w_ref, out_refs):
    depth, _, _, width = w_ref.shape
    chunk = pick_ref.shape[0] // ROLES
    span = 2 * ROLES * chunk
    flat = w_ref.reshape(depth * ROLES * 2, width)
    for i in range(depth // chunk):
        found = jnp.dot(pick_ref[...], flat[i * span : (i + 1) * span, :], preferred_element_type=jnp.float32)
        found = found.astype(jnp.bfloat16)
        for r in range(ROLES):
            out_refs[r][i * chunk : (i + 1) * chunk, :] = found[r * chunk : (r + 1) * chunk]


CHUNK = 64


def early_kernel(count, rows, index_ref, tokens_ref, w_ref, out_weights_ref, flag_ref, *refs):
    outs, (held, weights_ref, pick_ref, x_ref, w_sems, out_sems, x_sems) = refs[:count], refs[count:]
    frames, _, depth = tokens_ref.shape
    block = held.shape[1]
    steps = depth // block

    def load(step):
        return pltpu.make_async_copy(w_ref.at[pl.ds(step * block, block)], held.at[step % SLOTS], w_sems.at[step % SLOTS])

    def store(step):
        here = pl.ds(step * block, block)
        return pltpu.make_async_copy(weights_ref.at[here], out_weights_ref.at[here], out_sems.at[step])

    for step in range(SLOTS - 1):
        load(step).start()
    loads = []
    for i in range(count):
        start = pl.multiple_of(index_ref[i] * rows, rows)
        for f in range(frames):
            at = i * frames + f
            loads.append(
                pltpu.make_async_copy(
                    tokens_ref.at[f, pl.ds(start, rows)], x_ref.at[pl.ds(at * rows, rows)], x_sems.at[at]
                )
            )
            loads[-1].start()
    pick_ref[...] = pick_matrix(1, CHUNK)
    for step in range(steps):
        if step + SLOTS - 1 < steps:
            load(step + SLOTS - 1).start()
        load(step).wait()
        here = pl.ds(step * block, block)
        width = held.shape[-1]
        outs_at = [weights_ref.at[here, r * width : (r + 1) * width] for r in range(ROLES)]
        pick(pick_ref, held.at[step % SLOTS], outs_at)
        store(step).start()
    for copy in loads:
        copy.wait()
    total = jnp.dot(x_ref[...], weights_ref[...], preferred_element_type=jnp.float32)
    flag_ref[...] = jnp.zeros_like(flag_ref)
    for i, out in enumerate(outs):
        for pair in range(frames // 2):
            at = (i * frames + 2 * pair) * rows
            for g in range(rows // 8):
                out[g, pair * 16 : pair * 16 + 16, :] = pair_tiles(total, at, at + rows, g)
    for step in range(steps):
        store(step).wait()


def early(index, tokens, paired, rows, count):
    frames, _, depth = tokens.shape
    width = paired.shape[-1]
    cols = ROLES * width
    block = BLOCK
    out = jax.ShapeDtypeStruct((rows // 8, frames * 8, cols), jnp.bfloat16)
    here = count * frames * rows
    return pl.pallas_call(
        lambda *refs: early_kernel(count, rows, *refs),
        in_specs=[pl.BlockSpec(memory_space=pltpu.SMEM)] + [pl.BlockSpec(memory_space=pl.ANY)] * 2,
        out_specs=[pl.BlockSpec(memory_space=pl.ANY)] + [VMEM] * (1 + count),
        out_shape=[pltpu.HBM((depth, cols), jnp.bfloat16), jax.ShapeDtypeStruct((8, HD), jnp.float32)] + [out] * count,
        scratch_shapes=[
            pltpu.VMEM((SLOTS, block, ROLES, 2, width), jnp.bfloat16),
            pltpu.VMEM((depth, cols), jnp.bfloat16),
            pltpu.VMEM((ROLES * CHUNK, 2 * ROLES * CHUNK), jnp.bfloat16),
            pltpu.VMEM((here, depth), jnp.bfloat16),
            pltpu.SemaphoreType.DMA((SLOTS,)),
            pltpu.SemaphoreType.DMA((depth // block,)),
            pltpu.SemaphoreType.DMA((count * frames,)),
        ],
        compiler_params=PARAMS,
        cost_estimate=LARGE,
        name="early",
    )(index, in_hbm(tokens), in_hbm(paired))


BLOCK = 512
SLOTS = 3
SPLITS = 3


def space_peak_kernel(heads, x_hbm, w_hbm, flag_ref, parts_hbm, last_hbm, peak_ref, *scratch):
    held, x_ref, weights_ref, last_ref, parts_ref, pick_ref, w_sems, x_sem, last_sem, parts_sem = scratch
    frames, positions, depth = x_hbm.shape
    steps, block = held.shape[:2]
    width = heads * HD
    loads = [pltpu.make_async_copy(w_hbm.at[pl.ds(i * block, block)], held.at[i], w_sems.at[i]) for i in range(steps)]
    for load in loads:
        load.start()
    load_tokens = pltpu.make_async_copy(x_hbm, x_ref, x_sem.at[0])
    load_tokens.start()
    pick_ref[...] = pick_matrix(0, CHUNK)
    for step in range(steps):
        loads[step].wait()
        here = pl.ds(step * block, block)
        outs = [weights_ref.at[here, r * width : (r + 1) * width] for r in range(2)] + [last_ref.at[here]]
        pick(pick_ref, held.at[step], outs)
    store_last = pltpu.make_async_copy(last_ref, last_hbm, last_sem.at[0])
    store_last.start()
    load_tokens.wait()
    tokens = x_ref[...].reshape(frames * positions, depth)
    parts_ref[...] = jnp.dot(tokens, weights_ref[...], preferred_element_type=jnp.float32).astype(jnp.bfloat16)
    store = pltpu.make_async_copy(parts_ref, parts_hbm, parts_sem.at[0])
    store.start()
    for h in range(heads):
        peak = jnp.full((1, 1), -jnp.inf, jnp.float32)
        for f in range(frames):
            query_part, key_part = (
                parts_ref[f * positions : (f + 1) * positions, r * width + h * HD : r * width + (h + 1) * HD]
                for r in range(2)
            )
            peak = jnp.maximum(peak, jnp.max(dot_nt(query_part, key_part), keepdims=True))
        peak_ref[:, h * HD : (h + 1) * HD] = jnp.broadcast_to(peak * score_scale, (8, HD))
    store.wait()
    store_last.wait()


def space_peak(tokens, paired, flag, heads):
    frames, positions, depth = tokens.shape
    width = heads * HD
    rows = frames * positions
    block = BLOCK
    place = pl.BlockSpec(memory_space=pl.ANY)
    return pl.pallas_call(
        lambda *refs: space_peak_kernel(heads, *refs),
        in_specs=[place] * 3,
        out_specs=[place, place, VMEM],
        out_shape=[
            pltpu.HBM((rows, 2 * width), jnp.bfloat16),
            pltpu.HBM((depth, width), jnp.bfloat16),
            jax.ShapeDtypeStruct((8, width), jnp.float32),
        ],
        scratch_shapes=[
            pltpu.VMEM((depth // block, block, ROLES, 2, width), jnp.bfloat16),
            pltpu.VMEM(tokens.shape, jnp.bfloat16),
            pltpu.VMEM((depth, 2 * width), jnp.bfloat16),
            pltpu.VMEM((depth, width), jnp.bfloat16),
            pltpu.VMEM((rows, 2 * width), jnp.bfloat16),
            pltpu.VMEM((ROLES * CHUNK, 2 * ROLES * CHUNK), jnp.bfloat16),
            pltpu.SemaphoreType.DMA((depth // block,)),
            pltpu.SemaphoreType.DMA((1,)),
            pltpu.SemaphoreType.DMA((1,)),
            pltpu.SemaphoreType.DMA((1,)),
        ],
        compiler_params=pltpu.CompilerParams(vmem_limit_bytes=46 * 1024 * 1024),
        cost_estimate=SMALL,
        name="space_peak",
    )(in_hbm(tokens), in_hbm(paired), flag)


def space_kernel(heads, x_hbm, w_ref, parts_hbm, out_hbm, x_ref, parts_ref, out_ref, total, x_sems, parts_sem, out_sems):
    frames, positions, depth = x_hbm.shape
    width = heads * HD
    span = depth // SPLITS
    loads = []
    for split in range(SPLITS):
        here = pl.ds(split * span, span)
        loads.append([pltpu.make_async_copy(x_hbm.at[:, :, here], x_ref.at[:, :, here], x_sems.at[split])])
    loads.append([pltpu.make_async_copy(parts_hbm, parts_ref, parts_sem.at[0])])
    for group in loads:
        for copy in group:
            copy.start()
    for split in range(SPLITS):
        for copy in loads[split]:
            copy.wait()
        at = split * span
        tokens = x_ref[:, :, at : at + span].reshape(frames * positions, span)
        part = jnp.dot(tokens, w_ref[at : at + span, :], preferred_element_type=jnp.float32)
        total[...] = part if split == 0 else total[...] + part
    loads[-1][0].wait()
    stores = []
    for f in range(frames):
        rows = slice(f * positions, (f + 1) * positions)
        for h in range(heads):
            cols = [parts_ref[rows, r * width + h * HD : r * width + (h + 1) * HD] for r in range(2)]
            result, _ = attend(*cols, total[rows, h * HD : (h + 1) * HD].astype(jnp.bfloat16))
            out_ref[f, :, h * HD : (h + 1) * HD] = result.astype(jnp.bfloat16)
        stores.append(pltpu.make_async_copy(out_ref.at[f], out_hbm.at[f], out_sems.at[f]))
        stores[-1].start()
    for store in stores:
        store.wait()


def space_attention(tokens, weights, parts, heads):
    frames, positions, depth = tokens.shape
    width = heads * HD
    rows = frames * positions
    place = pl.BlockSpec(memory_space=pl.ANY)
    return pl.pallas_call(
        lambda *refs: space_kernel(heads, *refs),
        in_specs=[place, VMEM, place],
        out_specs=place,
        out_shape=jax.ShapeDtypeStruct((frames, positions, width), jnp.bfloat16),
        scratch_shapes=[
            pltpu.VMEM(tokens.shape, jnp.bfloat16),
            pltpu.VMEM((rows, 2 * width), jnp.bfloat16),
            pltpu.VMEM((frames, positions, width), jnp.bfloat16),
            pltpu.VMEM((rows, width), jnp.float32),
            pltpu.SemaphoreType.DMA((SPLITS,)),
            pltpu.SemaphoreType.DMA((1,)),
            pltpu.SemaphoreType.DMA((frames,)),
        ],
        compiler_params=PARAMS,
        cost_estimate=LARGE,
        name="space_attention",
    )(in_hbm(tokens), pltpu.with_memory_space_constraint(weights, pltpu.VMEM), in_hbm(parts))


def pieces(value):
    high = value.astype(jnp.bfloat16).astype(jnp.float32)
    mid = (value - high).astype(jnp.bfloat16).astype(jnp.float32)
    return high, mid, value - high - mid


def pair_tiles(total, one, two, group):
    tile = jnp.concatenate([total[at + group * 8 : at + group * 8 + 8] for at in (one, two)], axis=0)
    return tile.astype(jnp.bfloat16)


def project_kernel(blocks, rows, one_ref, two_ref, w_ref, out_ref):
    tokens = jnp.concatenate([one_ref[...], two_ref[...]], axis=0)
    total = jnp.dot(tokens, w_ref[...], preferred_element_type=jnp.float32)
    for g in range(rows // 8):
        for b in range(blocks):
            out_ref[g, b * 16 : b * 16 + 16, :] = pair_tiles(total, b * rows, (blocks + b) * rows, g)


def project(one, two, weights):
    blocks, rows, depth = one.shape
    return pl.pallas_call(
        lambda *refs: project_kernel(blocks, rows, *refs),
        in_specs=[VMEM] * 3,
        out_specs=VMEM,
        out_shape=jax.ShapeDtypeStruct((rows // 8, blocks * 16, weights.shape[1]), jnp.bfloat16),
        compiler_params=PARAMS,
        cost_estimate=LARGE,
        name="project",
    )(*[x.reshape(-1, depth) for x in (one, two)], pltpu.with_memory_space_constraint(weights, pltpu.VMEM))


def late_kernel(heads, spots, blocks_to, rows, *refs):
    (one_ref, two_ref, w_ref), ins, peak_ref = refs[:3], refs[3 : 3 + len(spots)], refs[3 + len(spots)]
    outs, parts_ref = refs[4 + len(spots) : -1], refs[-1]
    half = outs[0].shape[0]
    outs = [*outs[:2], outs[2].at[pl.ds(0, half)], outs[2].at[pl.ds(half, half)], *outs[3:]]
    blocks = len(blocks_to)
    tokens = jnp.concatenate([one_ref[...], two_ref[...]], axis=0)
    total = jnp.dot(tokens, w_ref[...], preferred_element_type=jnp.float32)
    for b in range(blocks):
        for g in range(rows // 8):
            parts_ref[g, b * 16 : b * 16 + 16, :] = pair_tiles(total, b * rows, (blocks + b) * rows, g)
    places = [place for spot in spots for place in spot] + [(d, 1) for d in blocks_to]
    attend_time(heads, places, [*ins, parts_ref], peak_ref, outs)


def attend_time(heads, spots, ins, peak_ref, outs):
    groups = ins[0].shape[0]
    width = heads * HD
    size = 16 * len(spots)
    row = lax.broadcasted_iota(jnp.int32, (size, size), 0)
    col = lax.broadcasted_iota(jnp.int32, (size, size), 1)
    mask = ((row ^ col) & 7) == 0
    line = lax.broadcasted_iota(jnp.int32, (16, HD), 0)
    lane = lax.broadcasted_iota(jnp.int32, (16, HD), 1) // TAIL
    tail = jnp.zeros((16, HD), jnp.float32)
    for h in range(heads):
        peak = jnp.full((1, 1), -jnp.inf, jnp.float32)
        results = []
        for g in range(groups):
            cols = []
            for r in range(ROLES):
                at = r * width + h * HD
                cols.append(jnp.concatenate([x[g, :, at : at + HD] for x in ins], axis=0))
            result, highest = attend(*cols, mask)
            peak = jnp.maximum(peak, highest * score_scale)
            results.append(result)
        for i, (out, pair) in enumerate(spots):
            for two in range(0, groups, 2):
                for k in range(2):
                    at = i * 16 + k * 8
                    tile = jnp.concatenate([results[two + j][at : at + 8] for j in range(2)], axis=0)
                    start = ((h * 4 + 2 * pair + k) * groups + two) * 8
                    outs[out][start : start + 16, :] = tile.astype(jnp.bfloat16)
        both = pieces(peak_ref[0:1, h * HD : (h + 1) * HD]) + pieces(jnp.broadcast_to(peak, (1, HD)))
        for i, value in enumerate(both):
            tail = jnp.where((line == i) & (lane == h), value, tail)
    for out in outs:
        out[heads * groups * 32 :, :] = tail.astype(jnp.bfloat16)


TAIL = 32


def late(one, two, weights, parts, spots, peaks, heads, count, blocks_to):
    blocks, rows, depth = one.shape
    cols = weights.shape[1]
    groups = rows // 8
    shape = (heads * groups * 32 + 16, HD)
    return pl.pallas_call(
        lambda *refs: late_kernel(heads, spots, blocks_to, rows, *refs),
        in_specs=[VMEM] * (4 + len(parts)),
        out_specs=[VMEM] * (count - 1),
        out_shape=[jax.ShapeDtypeStruct(shape, jnp.bfloat16)] * 2
        + [jax.ShapeDtypeStruct((2 * shape[0], HD), jnp.bfloat16)]
        + [jax.ShapeDtypeStruct(shape, jnp.bfloat16)] * (count - 4),
        scratch_shapes=[
            pltpu.VMEM((groups, blocks * 16, cols), jnp.bfloat16),
        ],
        compiler_params=PARAMS,
        cost_estimate=LARGE,
        name="late",
    )(
        *[x.reshape(-1, depth) for x in (one, two)],
        pltpu.with_memory_space_constraint(weights, pltpu.VMEM),
        *parts,
        peaks,
    )


def finish_kernel(direct, heads, index_ref, *refs):
    ins, out_ref, clip_ref = refs[:-2], refs[-2], refs[-1]
    half = ins[0].shape[0]
    near = [ins[0], ins[1].at[pl.ds(0, half)], ins[2].at[pl.ds(0, half)], ins[2].at[pl.ds(half, half)]]
    ins = [*near, *ins[3:]]
    rows = (half - 16) // (4 * heads)
    mine = index_ref[0]
    peak = None
    for d, source in enumerate(ins):
        start = pl.multiple_of(index_ref[1 + d] * rows, rows)
        for h in range(heads):
            for pair in range(2):
                for k in range(2):
                    frame = 2 * pair + k if d in direct else mine ^ (pair + 2 * k)
                    at = (h * 4 + 2 * pair + k) * rows
                    out_ref[frame, pl.ds(start, rows), h * HD : (h + 1) * HD] = source[at : at + rows, :]
        tail = source[half - 16 :, :].astype(jnp.float32)
        values = [tail[3 * a : 3 * a + 1] + tail[3 * a + 1 : 3 * a + 2] + tail[3 * a + 2 : 3 * a + 3] for a in range(2)]
        peak = values if peak is None else [jnp.maximum(p, v) for p, v in zip(peak, values)]
    for a in range(2):
        clip = jnp.sqrt(clip_limit / jnp.maximum(peak[a], clip_limit))
        clip_ref[a : a + 1, :] = jnp.concatenate([clip[:, h * TAIL : h * TAIL + 1] for h in range(heads)], axis=1)


def finish(index, received, frames, positions, direct, heads):
    return pl.pallas_call(
        lambda *refs: finish_kernel(direct, heads, *refs),
        in_specs=[pl.BlockSpec(memory_space=pltpu.SMEM)] + [VMEM] * len(received),
        out_specs=[VMEM, VMEM],
        out_shape=[
            jax.ShapeDtypeStruct((frames, positions, heads * HD), jnp.bfloat16),
            jax.ShapeDtypeStruct((2, heads), jnp.float32),
        ],
        compiler_params=PARAMS,
        name="finish",
    )(index, *received)


def swap(value, axis, size, distance):
    return lax.ppermute(value, axis, [(i, i ^ distance) for i in range(size)])


def fast_body(seq, head, patch_tokens, projection):
    frames, positions, depth = patch_tokens.shape
    heads = projection.shape[-1] // HD
    width = heads * HD
    rows = positions // seq
    me, mine = lax.axis_index("seq"), lax.axis_index("head")
    token_group, direct = (3, 2, 5, 4), (1, 7, 6)
    paired = jnp.transpose(projection, (0, 2, 1, 3))

    def piece(frame, owner):
        return lax.dynamic_slice(patch_tokens, (frame, owner * rows, 0), (1, rows, depth))

    got = [swap(piece(mine, me ^ d), "seq", seq, d) for d in token_group]
    index = jnp.stack([me ^ d for d in (*direct, 0)]).astype(jnp.int32)
    weights, flag, *away, own = early(index, patch_tokens, paired, rows, len(direct) + 1)
    away = [swap(part, "seq", seq, d) for d, part in zip(direct, away)]

    *got, flag = lax.optimization_barrier([*got, flag])
    here = jnp.concatenate(got, axis=0)
    there = swap(here, "head", head, 2)
    parts, last, peaks = space_peak(patch_tokens, paired, flag, heads)
    here, there, peaks = lax.optimization_barrier([here, there, peaks])
    here_other = swap(here, "head", head, 1)
    there_other = swap(there, "head", head, 1)
    first = project(here, there, weights)
    spots = [[(d, 0), (d, 1)] for d in (*direct, 0)] + [[(d, 0) for d in token_group]]
    outs = late(here_other, there_other, weights, [*away, own, first], spots, peaks, heads, seq, token_group)
    *outs, parts = lax.optimization_barrier([*outs, parts])
    mine_out, x_out, z_out, *far_outs = outs
    half = mine_out.shape[0]
    z_pair = swap(z_out, "seq", seq, 2)
    far_pairs = [swap(out, "seq", seq, d) for d, out in zip((4, 5, 6, 7), far_outs)]
    x_pair = swap(jnp.concatenate([x_out, z_pair[half:]], axis=0), "seq", seq, 1)
    received = [mine_out, z_pair, x_pair, *far_pairs]
    order = (0, 2, 1, 3, 4, 5, 6, 7)
    space_out = space_attention(patch_tokens, last, parts, heads)
    finish_index = jnp.stack([mine] + [me ^ d for d in order]).astype(jnp.int32)
    natural = [i for i, d in enumerate(order) if d not in token_group]
    time_out, clip = finish(finish_index, received, frames, positions, natural, heads)
    return space_out, time_out, clip


def mixing(scores):
    highest = jnp.max(scores, axis=-1, keepdims=True)
    expon = jnp.exp(scores - highest)
    return (expon / jnp.sum(expon, axis=-1, keepdims=True)).astype(jnp.bfloat16)


def plain_attention(form, query_part, key_part, value_part):
    scores = jnp.einsum(form[0], query_part, key_part, preferred_element_type=jnp.float32) * score_scale
    result = jnp.einsum(form[1], mixing(scores), value_part, preferred_element_type=jnp.float32)
    return result.astype(jnp.bfloat16), jnp.max(scores, axis=(0, 2, 3))


def plain_body(patch_tokens, projection):
    frames, positions, depth = patch_tokens.shape
    heads = projection.shape[-1] // HD
    parts = jnp.dot(
        patch_tokens.reshape(-1, depth), projection.reshape(depth, -1), preferred_element_type=jnp.float32
    )
    parts = parts.astype(jnp.bfloat16).reshape(frames, positions, 2, ROLES, heads, HD)
    space_out, space_high = plain_attention(
        ("fihd,fjhd->fhij", "fhij,fjhd->fihd"), *(parts[:, :, 0, r] for r in range(ROLES))
    )
    moved = [lax.all_to_all(parts[:, :, 1, r], "seq", split_axis=1, concat_axis=0, tiled=True) for r in range(ROLES)]
    time_out, time_high = plain_attention(("fphd,gphd->phfg", "phfg,gphd->fphd"), *moved)
    time_out = lax.all_to_all(time_out, "seq", split_axis=0, concat_axis=1, tiled=True)
    peak = lax.pmax(jnp.stack([space_high, time_high]), "seq")
    clip_factor = jnp.sqrt(clip_limit / jnp.maximum(peak, clip_limit))
    flat = (frames, positions, heads * HD)
    return space_out.reshape(flat), time_out.reshape(flat), clip_factor


def solution(mesh):
    seq, head = mesh.shape["seq"], mesh.shape["head"]

    def body(patch_tokens, projection):
        frames, positions, _ = patch_tokens.shape
        if seq == 8 and head == 4 and frames == 4 and positions % (16 * seq) == 0 and projection.shape[-1] <= 4 * HD:
            return fast_body(seq, head, patch_tokens, projection)
        return plain_body(patch_tokens, projection)

    return jax.shard_map(
        body,
        mesh=mesh,
        in_specs=(P("seq", None, None), P(None, None, None, "head")),
        out_specs=(P("seq", None, "head"), P("seq", None, "head"), P(None, "head")),
        check_vma=False,
    )
```
